128 devices in a mesh: tok: 4 (over x), vocab: 32 (over y, z, core).
Axes of the slice: x: 4, y: 4, z: 4, core: 2. Of those that a mesh axis runs over, the one named last changes fastest.
Arguments:
- hidden: bfloat16 [1024, 4096], P('tok', 'vocab'), may hold values from -64 to 64
- head_weight: bfloat16 [4096, 77824], P(None, 'vocab'), may hold values from -2 to 2
- teacher_logits: bfloat16 [256, 4, 77824], P('vocab', None, 'tok'), may hold values from -18 to 300
- token_ids: int32 [1024], P('tok'), may hold values from 0 to 77823
- token_weight: float32 [1024], P('tok'), may hold values from 8 to 80
Outputs:
- divergence: float32 [1024], P('tok')
- cross_entropy: float32 [1024], P('tok')
- hidden_grad: bfloat16 [4096, 1024], P('vocab', 'tok')
The draws below stay inside these ranges and needn't reach their ends.
All inputs are finite; a program needn't handle non-finite values.
Results may differ from the reference program's by a relative error of at most 0.02.
Values may be sent and summed in bfloat16 or wider, within the bound.
No kernel may reach another device: no remote copies, remote signals or barrier semaphores. Data moves between devices by JAX's collectives and lax.ppermute only.
A program may use at most 192 MiB of HBM per device.

```python
import math
import jax
import jax.numpy as jnp
from jax import lax

D = 4096
VOCAB = 77824
TOK_DEV = 256
TOKENS = 1024
N_TOK = 4


def shared_field(key):
    return jnp.clip(jax.random.normal(jax.random.fold_in(key, 902), (D, VOCAB), jnp.float32), -5.0, 5.0)


def draw_head_weight(key, part):
    field = shared_field(key)
    return (field * (3.0 / math.sqrt(D))).astype(jnp.bfloat16)


def draw_hidden(key, part):
    key = jax.random.fold_in(key, 5)
    values = jnp.clip(jax.random.normal(key, (TOKENS, D), jnp.float32), -6.0, 6.0)
    return values.astype(jnp.bfloat16)


def draw_teacher_logits(key, part):
    key = jax.random.fold_in(key, 7)
    values = jnp.clip(3.0 * jax.random.normal(key, (TOK_DEV, N_TOK, VOCAB), jnp.float32), -18.0, 18.0)
    return values.astype(jnp.bfloat16)


def plant(values, rng, least, top_value):
    dims = values.shape
    index_at = [jax.random.randint(jax.random.fold_in(rng, axis), (), 0, dims[axis]) for axis in range(len(dims))]
    values = values.at[tuple(index_at)].set(least)
    longest = dims.index(max(dims))
    index_at[longest] = (index_at[longest] + 1) % dims[longest]
    return values.at[tuple(index_at)].set(top_value)


def block_scale(key, shape, pieces, low, high):
    def one(position, shards_of):
        draws = jax.random.uniform(jax.random.fold_in(jax.random.fold_in(key, 6), position), (shards_of,), jnp.float32, low / len(pieces), high / len(pieces))
        return jnp.repeat(jnp.exp(draws), shape[position] // shards_of).reshape((-1,) + (1,) * (len(shape) - position - 1))

    level = one(*pieces[0])
    for cut in pieces[1:]:
        level = level * one(*cut)
    return level


def setup_inputs(seed: int = 0) -> dict:
    key_list = jax.random.split(jax.random.key(seed), 6)
    return {
        "hidden": draw_hidden(jax.random.fold_in(key_list[5], 71), 0),
        "head_weight": draw_head_weight(jax.random.fold_in(key_list[5], 71), 0),
        "teacher_logits": draw_teacher_logits(jax.random.fold_in(key_list[5], 71), 0),
        "token_ids": plant(jax.random.randint(key_list[3], (TOKENS,), 0, VOCAB), jax.random.fold_in(key_list[3], 1), 0, VOCAB - 1).astype(jnp.int32),
        "token_weight": jnp.clip(jnp.exp(math.log(80.0) - 2.3025851 * jax.random.uniform(key_list[4], (TOKENS,), jnp.float32) ** block_scale(key_list[4], (TOKENS,), ((0, 4),), -0.2, 0.2)), 8.0, 80.0),
    }


CE_WEIGHT = 0.5


def reference(hidden, head_weight, teacher_logits, token_ids, token_weight):
    teacher = jnp.transpose(teacher_logits, (1, 0, 2)).reshape(TOKENS, VOCAB).astype(jnp.float32)
    student = jnp.dot(hidden, head_weight, preferred_element_type=jnp.float32)
    student_lse = jax.nn.logsumexp(student, axis=1)
    teacher_lse = jax.nn.logsumexp(teacher, axis=1)
    student_logp = student - student_lse[:, None]
    teacher_logp = teacher - teacher_lse[:, None]
    student_prob = jnp.exp(student_logp)
    teacher_prob = jnp.exp(teacher_logp)
    divergence = jnp.sum(teacher_prob * (teacher_logp - student_logp), axis=1)
    picked = jnp.take_along_axis(student, token_ids[:, None].astype(jnp.int32), axis=1)[:, 0]
    cross_entropy = student_lse - picked
    onehot = (jnp.arange(VOCAB, dtype=jnp.int32)[None, :] == token_ids[:, None]).astype(jnp.float32)
    logit_grad = (token_weight[:, None] * ((student_prob - teacher_prob) + CE_WEIGHT * (student_prob - onehot))).astype(jnp.bfloat16)
    hidden_grad = lax.dot_general(head_weight, logit_grad, (((1,), (1,)), ((), ())), preferred_element_type=jnp.float32)
    return divergence, cross_entropy, hidden_grad.astype(jnp.bfloat16)
```

```python
import functools

import jax
import jax.numpy as jnp
from jax import lax
from jax.experimental import pallas as pl
from jax.experimental.pallas import tpu as pltpu
from jax.sharding import PartitionSpec as P

CE_WEIGHT = 0.5
RING = 4
CHIPS = RING * RING
SHIFTS = (0, 1, -1, 2)
MIB = 1 << 20
TAIL = 16


def params(limit):
    return pltpu.CompilerParams(vmem_limit_bytes=limit * MIB)


def cost(flops, read):
    return pl.CostEstimate(flops=flops, bytes_accessed=read, transcendentals=0)


def member(y, z, core):
    return ((y % RING) * RING + z % RING) * 2 + core % 2


def moves(dy=0, dz=0, dcore=0):
    return [
        (member(y, z, c), member(y + dy, z + dz, c + dcore))
        for y in range(RING)
        for z in range(RING)
        for c in range(2)
    ]


def swap_core(x):
    return lax.ppermute(x, "vocab", moves(dcore=1))


def from_ring(x, axis):
    return [x] + [lax.ppermute(x, "vocab", moves(**{axis: d})) for d in SHIFTS[1:]]


def eye(n):
    return lax.broadcasted_iota(jnp.int32, (n, n), 0) == lax.broadcasted_iota(jnp.int32, (n, n), 1)


def to_column(row):
    n = row.shape[1]
    return jnp.sum(jnp.where(eye(n), row, 0.0), axis=1, keepdims=True)


def to_row(column):
    n = column.shape[0]
    return jnp.sum(jnp.where(eye(n), column, 0.0), axis=0, keepdims=True)


def relayout_kernel(x_ref, o_ref):
    for b in range(x_ref.shape[1]):
        o_ref[b, 0] = x_ref[:, b, :]


def relayout(teacher_logits, local_vocab):
    rows, tiles, width = teacher_logits.shape
    shards = width // local_vocab
    return pl.pallas_call(
        relayout_kernel,
        grid=(shards,),
        in_specs=[pl.BlockSpec((rows, tiles, local_vocab), lambda i: (0, 0, i))],
        out_specs=pl.BlockSpec((tiles, 1, rows, local_vocab), lambda i: (0, i, 0, 0)),
        out_shape=jax.ShapeDtypeStruct((tiles, shards, rows, local_vocab), jnp.bfloat16),
        compiler_params=params(16),
        name="teacher_relayout",
    )(teacher_logits)


def teacher_lse_kernel(where_ref, x_ref, o_ref, acc):
    pairs = x_ref.shape[0] // 16

    def block(i):
        x = x_ref[pl.ds(pl.multiple_of(i * 16, 16), 16), :].astype(jnp.float32)
        return x[:8], x[8:]

    first, second = block(0)
    acc[...] = jnp.maximum(first, second)

    def widen(i, _):
        a, b = block(i)
        acc[...] = jnp.maximum(acc[...], jnp.maximum(a, b))
        return 0

    lax.fori_loop(1, pairs, widen, 0)
    top = jnp.max(acc[...], axis=1, keepdims=True)
    acc[...] = jnp.zeros_like(acc)

    def add(i, _):
        a, b = block(i)
        acc[...] += jnp.exp(a - top) + jnp.exp(b - top)
        return 0

    lax.fori_loop(0, pairs, add, 0)
    lse = top + jnp.log(jnp.sum(acc[...], axis=1, keepdims=True))
    lane = lax.broadcasted_iota(jnp.int32, o_ref.shape, 1)
    row = lax.broadcasted_iota(jnp.int32, o_ref.shape, 0)
    placed = jnp.where(lane == where_ref[0] * 8 + row, lse, 0.0)
    o_ref[...] = jnp.broadcast_to(jnp.sum(placed, axis=0, keepdims=True), o_ref.shape)


def teacher_lse(rows, where):
    n, width = rows.shape
    return pl.pallas_call(
        teacher_lse_kernel,
        grid_spec=pltpu.PrefetchScalarGridSpec(
            num_scalar_prefetch=1,
            grid=(1,),
            in_specs=[pl.BlockSpec((n, width), lambda i, m: (0, 0))],
            out_specs=pl.BlockSpec((8, n), lambda i, m: (0, 0)),
            scratch_shapes=[pltpu.VMEM((8, width), jnp.float32)],
        ),
        out_shape=jax.ShapeDtypeStruct((8, n), jnp.float32),
        compiler_params=params(16),
        name="teacher_lse",
    )(where, rows)


BLOCK = 512


def student_kernel(width, meta_ref, *refs):
    own, other = refs[0:RING], refs[RING : 2 * RING]
    w_ref, lse_ref, s_ref, stat_ref, hidden, peak, total = refs[2 * RING :]
    step = pl.program_id(0)
    rows = hidden.shape[0]

    @pl.when(step == 0)
    def _():
        core = meta_ref[0]
        for i in range(CHIPS):
            at = slice((i % RING) * rows, (i % RING + 1) * rows)
            chip = meta_ref[1 + i]
            hidden[:, pl.ds(pl.multiple_of((chip * 2 + core) * 128, 128), 128)] = own[i // RING][at, :]
            hidden[:, pl.ds(pl.multiple_of((chip * 2 + 1 - core) * 128, 128), 128)] = other[i // RING][at, :]
        peak[...] = jnp.full_like(peak, -jnp.inf)
        total[...] = jnp.zeros_like(total)

    s = jnp.dot(hidden[...], w_ref[...], preferred_element_type=jnp.float32)
    s_ref[...] = s
    column = step * BLOCK + lax.broadcasted_iota(jnp.int32, s.shape, 1)
    s = jnp.where(column < width, s, -jnp.inf)
    old = peak[:, :1]
    new = jnp.maximum(old, jnp.max(s, axis=1, keepdims=True))
    sums = total[:, :1] * jnp.exp(old - new) + jnp.sum(jnp.exp(s - new), axis=1, keepdims=True)
    peak[...] = jnp.broadcast_to(new, peak.shape)
    total[...] = jnp.broadcast_to(sums, total.shape)

    @pl.when(step == pl.num_programs(0) - 1)
    def _():
        row = lax.broadcasted_iota(jnp.int32, stat_ref.shape, 0)
        stat_ref[...] = jnp.where(
            row == 0, to_row(peak[:, :1]), jnp.where(row == 1, to_row(total[:, :1]), lse_ref[...])
        )


def student_logits(meta, own, other, head_weight, lse_rows):
    depth, width = head_weight.shape
    rows = own[0].shape[0] // RING
    steps = pl.cdiv(width, BLOCK)
    whole = pl.BlockSpec((RING * rows, 128), lambda i, m: (0, 0))
    return pl.pallas_call(
        functools.partial(student_kernel, width),
        grid_spec=pltpu.PrefetchScalarGridSpec(
            num_scalar_prefetch=1,
            grid=(steps,),
            in_specs=[whole] * (2 * RING)
            + [
                pl.BlockSpec((depth, BLOCK), lambda i, m: (0, i)),
                pl.BlockSpec((8, rows), lambda i, m: (0, 0)),
            ],
            out_specs=[
                pl.BlockSpec((rows, BLOCK), lambda i, m: (0, i)),
                pl.BlockSpec((8, rows), lambda i, m: (0, 0)),
            ],
            scratch_shapes=[
                pltpu.VMEM((rows, depth), jnp.bfloat16),
                pltpu.VMEM((rows, 128), jnp.float32),
                pltpu.VMEM((rows, 128), jnp.float32),
            ],
        ),
        out_shape=[
            jax.ShapeDtypeStruct((rows, width), jnp.float32),
            jax.ShapeDtypeStruct((8, rows), jnp.float32),
        ],
        compiler_params=params(40),
        cost_estimate=cost(2 * rows * depth * width, 2 * depth * width),
        name="student_logits",
    )(meta, *own, *other, head_weight, lse_rows)


def ring_sum(parts):
    return (parts[0] + parts[3]) + (parts[1] + parts[2])


def split_bf16(x):
    high = x.astype(jnp.bfloat16).astype(jnp.float32)
    rest = x - high
    middle = rest.astype(jnp.bfloat16).astype(jnp.float32)
    return high, middle, rest - middle


def grad_matmul(w_ref, grad):
    chips, share, width = w_ref.shape[0], w_ref.shape[2], w_ref.shape[3]
    out = lax.dot_general(
        w_ref[...].reshape(chips * share, width),
        grad,
        (((1,), (1,)), ((), ())),
        preferred_element_type=jnp.float32,
    )
    return out.astype(jnp.bfloat16).reshape(chips, share, grad.shape[0])


ROWS = 32


def grad_kernel(meta_ref, *refs):
    stats = refs[0:RING]
    s_ref, t_ref, id_ref, weight_ref, w_ref, grad_ref, part_ref, tail_ref, column, sums = refs[RING:]

    @pl.when(pl.program_id(0) == 0)
    def _():
        rows, width = s_ref.shape

        def pick(i, j, k, row):
            at = (j * 2 + k) * 8 + row
            return stats[i][at : at + 1, :]

        grid = [(i, j, k) for i in range(RING) for j in range(RING) for k in range(2)]
        top = functools.reduce(jnp.maximum, [pick(*g, 0) for g in grid])
        share = {g: pick(*g, 1) * jnp.exp(pick(*g, 0) - top) for g in grid}
        total = ring_sum(
            [ring_sum([share[i, j, 0] + share[i, j, 1] for j in range(RING)]) for i in range(RING)]
        )
        teacher_row = functools.reduce(jnp.add, [pick(*g, 2) for g in grid])
        column[:, 0:1] = to_column(top + jnp.log(total))
        column[:, 1:2] = to_column(teacher_row)
        column[:, 2:3] = to_column(weight_ref[...])
        column[:, 3:4] = to_column(id_ref[...].astype(jnp.float32))
        first = meta_ref[1]

        def chunk(i, _):
            at = pl.ds(pl.multiple_of(i * ROWS, ROWS), ROWS)
            student_lse, teacher_lse = column[at, 0:1], column[at, 1:2]
            weight = column[at, 2:3]
            target = column[at, 3:4].astype(jnp.int32) - first
            lane = lax.broadcasted_iota(jnp.int32, (ROWS, 128), 1)
            cross = jnp.zeros((ROWS, 128), jnp.float32)
            picked = jnp.zeros((ROWS, 128), jnp.float32)
            for j in range(width // 128):
                cols = slice(j * 128, (j + 1) * 128)
                student_logp = s_ref[at, cols] - student_lse
                teacher_logp = t_ref[at, cols].astype(jnp.float32) - teacher_lse
                student_prob = jnp.exp(student_logp)
                teacher_prob = jnp.exp(teacher_logp)
                hit = lane == target - j * 128
                onehot = jnp.where(hit, 1.0, 0.0)
                cross += teacher_prob * (teacher_logp - student_logp)
                picked += jnp.where(hit, -student_logp, 0.0)
                grad = weight * ((student_prob - teacher_prob) + CE_WEIGHT * (student_prob - onehot))
                grad_ref[at, cols] = grad.astype(jnp.bfloat16)
            sums[at, 0:1] = jnp.sum(cross, axis=1, keepdims=True)
            sums[at, 1:2] = jnp.sum(picked, axis=1, keepdims=True)
            return 0

        lax.fori_loop(0, rows // ROWS, chunk, 0)
        lines = split_bf16(to_row(sums[:, 0:1])) + split_bf16(to_row(sums[:, 1:2]))
        row = lax.broadcasted_iota(jnp.int32, tail_ref.shape, 0)
        tail = jnp.zeros(tail_ref.shape, jnp.float32)
        for k, line in enumerate(lines):
            tail = jnp.where(row == k, line, tail)
        tail_ref[...] = tail.astype(jnp.bfloat16)

    part_ref[...] = grad_matmul(w_ref, grad_ref[...])


CHIP_BLOCK = 4


def logit_grad(meta, stats, student, teacher, ids, weights, shares):
    chips, cores, share, width = shares.shape
    rows = student.shape[0]
    whole = lambda shape: pl.BlockSpec(shape, lambda i, m: (0,) * len(shape))
    return pl.pallas_call(
        grad_kernel,
        grid_spec=pltpu.PrefetchScalarGridSpec(
            num_scalar_prefetch=1,
            grid=(chips // CHIP_BLOCK,),
            in_specs=[whole(stats[0].shape)] * RING
            + [
                whole((rows, width)),
                whole((rows, width)),
                whole((1, rows)),
                whole((1, rows)),
                pl.BlockSpec((CHIP_BLOCK, 1, share, width), lambda i, m: (i, 1 - m[0], 0, 0)),
            ],
            out_specs=[
                whole((rows, width)),
                pl.BlockSpec((CHIP_BLOCK, share, rows), lambda i, m: (i, 0, 0)),
                whole((TAIL, rows)),
            ],
            scratch_shapes=[
                pltpu.VMEM((rows, 128), jnp.float32),
                pltpu.VMEM((rows, 128), jnp.float32),
            ],
        ),
        out_shape=[
            jax.ShapeDtypeStruct((rows, width), jnp.bfloat16),
            jax.ShapeDtypeStruct((chips, share, rows), jnp.bfloat16),
            jax.ShapeDtypeStruct((TAIL, rows), jnp.bfloat16),
        ],
        compiler_params=params(40),
        cost_estimate=cost(rows * chips * share * width * 2, chips * share * width * 2),
        name="logit_grad",
    )(meta, *stats, student, teacher, ids, weights, shares)


def own_kernel(meta_ref, grad_ref, w_ref, part_ref):
    part_ref[...] = grad_matmul(w_ref, grad_ref[...])


def own_share(meta, grad, shares):
    chips, cores, share, width = shares.shape
    rows = grad.shape[0]
    return pl.pallas_call(
        own_kernel,
        grid_spec=pltpu.PrefetchScalarGridSpec(
            num_scalar_prefetch=1,
            grid=(chips // CHIP_BLOCK,),
            in_specs=[
                pl.BlockSpec((rows, width), lambda i, m: (0, 0)),
                pl.BlockSpec((CHIP_BLOCK, 1, share, width), lambda i, m: (i, m[0], 0, 0)),
            ],
            out_specs=pl.BlockSpec((CHIP_BLOCK, share, rows), lambda i, m: (i, 0, 0)),
        ),
        out_shape=jax.ShapeDtypeStruct((chips, share, rows), jnp.bfloat16),
        compiler_params=params(32),
        cost_estimate=cost(rows * chips * share * width * 2, chips * share * width * 2),
        name="own_share",
    )(meta, grad, shares)


def join_kernel(a_ref, b_ref, ta_ref, tb_ref, o_ref):
    share = a_ref.shape[1]
    total = a_ref[...].astype(jnp.float32) + b_ref[...].astype(jnp.float32)
    o_ref[:, 0:share, :] = total.astype(jnp.bfloat16)
    tail = jnp.concatenate(
        [ta_ref[...].astype(jnp.float32)[0 : TAIL // 2], tb_ref[...].astype(jnp.float32)[0 : TAIL // 2]]
    ).astype(jnp.bfloat16)
    for i in range(o_ref.shape[0]):
        o_ref[i, share : share + TAIL, :] = tail


def join(a, b, tail_a, tail_b):
    chips, share, rows = a.shape
    block = pl.BlockSpec((CHIP_BLOCK, share, rows), lambda i: (i, 0, 0))
    tail = pl.BlockSpec((TAIL, rows), lambda i: (0, 0))
    return pl.pallas_call(
        join_kernel,
        grid=(chips // CHIP_BLOCK,),
        in_specs=[block, block, tail, tail],
        out_specs=pl.BlockSpec((CHIP_BLOCK, share + TAIL, rows), lambda i: (i, 0, 0)),
        out_shape=jax.ShapeDtypeStruct((chips, share + TAIL, rows), jnp.bfloat16),
        compiler_params=params(16),
        name="chip_sum",
    )(a, b, tail_a, tail_b)


def final_kernel(x_ref, div_ref, ce_ref, o_ref):
    chips = x_ref.shape[0]
    share = x_ref.shape[1] - TAIL
    total = x_ref[0, 0:share, :].astype(jnp.float32)
    for i in range(1, chips):
        total += x_ref[i, 0:share, :].astype(jnp.float32)
    o_ref[...] = total.astype(jnp.bfloat16)
    div = jnp.zeros(div_ref.shape, jnp.float32)
    ce = jnp.zeros(ce_ref.shape, jnp.float32)
    for i in range(chips):
        tail = x_ref[i, share : share + TAIL, :].astype(jnp.float32)
        line = lambda k: tail[k : k + 1]
        value = lambda k: (line(k) + line(k + 1)) + line(k + 2)
        half = TAIL // 2
        div += value(0) + value(half)
        ce += value(3) + value(half + 3)
    div_ref[...] = div
    ce_ref[...] = ce


def final(blocks):
    chips, height, rows = blocks.shape
    return pl.pallas_call(
        final_kernel,
        out_shape=[
            jax.ShapeDtypeStruct((1, rows), jnp.float32),
            jax.ShapeDtypeStruct((1, rows), jnp.float32),
            jax.ShapeDtypeStruct((height - TAIL, rows), jnp.bfloat16),
        ],
        compiler_params=params(16),
        name="final_sum",
    )(blocks)


def on_device(hidden, head_weight, teacher_logits, token_ids, token_weight):
    rows, share = hidden.shape
    depth, width = head_weight.shape
    me = lax.axis_index("vocab")
    core, chip = me % 2, me // 2
    y, z = chip // RING, chip % RING
    sources = [((y - dy) % RING) * RING + (z - dz) % RING for dy in SHIFTS for dz in SHIFTS]

    along_z = jnp.concatenate(from_ring(hidden, "dz"), axis=0)
    own = from_ring(along_z, "dy")
    other = [swap_core(x) for x in own]

    blocks = relayout(teacher_logits, width).reshape(rows, width)
    blocks = lax.all_to_all(blocks, "tok", 0, 0, tiled=True)
    lse_rows = teacher_lse(blocks, me.reshape(1))
    teacher = lax.all_to_all(blocks, "vocab", 0, 0, tiled=True)

    meta = jnp.stack([core] + sources).astype(jnp.int32)
    student, stat = student_logits(meta, own, other, head_weight, lse_rows)
    stat = jnp.concatenate([stat, swap_core(stat)], axis=0)
    stats = from_ring(jnp.concatenate(from_ring(stat, "dz"), axis=0), "dy")

    meta = jnp.stack([core, me * width]).astype(jnp.int32)
    shares = head_weight.reshape(CHIPS, 2, share, width)
    grad, part, tail = logit_grad(
        meta, stats, student, teacher, token_ids.reshape(1, rows), token_weight.reshape(1, rows), shares
    )
    from_core, from_tail = swap_core(part), swap_core(tail)
    mine = own_share(meta, grad, shares)
    summed = join(mine, from_core, tail, from_tail)

    same_core = [[member(i // RING, i % RING, c) for i in range(CHIPS)] for c in range(2)]
    blocks = lax.all_to_all(
        summed.reshape(CHIPS * (share + TAIL), rows), "vocab", 0, 0, axis_index_groups=same_core, tiled=True
    )
    divergence, cross_entropy, hidden_grad = final(blocks.reshape(CHIPS, share + TAIL, rows))
    return divergence.reshape(rows), cross_entropy.reshape(rows), hidden_grad


def solution(mesh):
    return jax.shard_map(
        on_device,
        mesh=mesh,
        in_specs=(P("tok", "vocab"), P(None, "vocab"), P("vocab", None, "tok"), P("tok"), P("tok")),
        out_specs=(P("tok"), P("tok"), P("vocab", "tok")),
        check_vma=False,
    )
```

```python
import functools

import jax
import jax.numpy as jnp
from jax import lax
from jax.experimental import pallas as pl
from jax.experimental.pallas import tpu as pltpu
from jax.sharding import PartitionSpec as P

CE_WEIGHT = 0.5
RING = 4
CHIPS = RING * RING
SHIFTS = (0, 1, -1, 2)
MIB = 1 << 20
SMEM = pl.BlockSpec(memory_space=pltpu.SMEM)
VMEM = pl.BlockSpec(memory_space=pltpu.VMEM)
HBM = pl.BlockSpec(memory_space=pltpu.HBM)
TAIL = 16


def params(limit):
    return pltpu.CompilerParams(vmem_limit_bytes=limit * MIB)


def cost(flops, read):
    return pl.CostEstimate(flops=flops, bytes_accessed=read, transcendentals=0)


def in_vmem(x):
    return pltpu.with_memory_space_constraint(x, pltpu.VMEM)


def in_hbm(x):
    return pltpu.with_memory_space_constraint(x, pltpu.HBM)


def after(x, *others):
    return lax.optimization_barrier((x,) + others)[0]


def member(y, z, core):
    return ((y % RING) * RING + z % RING) * 2 + core % 2


def moves(dy=0, dz=0, dcore=0):
    return [
        (member(y, z, c), member(y + dy, z + dz, c + dcore))
        for y in range(RING)
        for z in range(RING)
        for c in range(2)
    ]


def swap_core(x):
    return lax.ppermute(x, "vocab", moves(dcore=1))


def from_ring(x, axis):
    return [x] + [lax.ppermute(x, "vocab", moves(**{axis: d})) for d in SHIFTS[1:]]


def eye(n):
    return lax.broadcasted_iota(jnp.int32, (n, n), 0) == lax.broadcasted_iota(jnp.int32, (n, n), 1)


def to_column(row):
    n = row.shape[1]
    return jnp.sum(jnp.where(eye(n), row, 0.0), axis=1, keepdims=True)


def to_row(column):
    n = column.shape[0]
    return jnp.sum(jnp.where(eye(n), column, 0.0), axis=0, keepdims=True)


def load_kernel(x_ref, o_ref, sem):
    copy = pltpu.make_async_copy(x_ref, o_ref, sem)
    copy.start()
    copy.wait()


def load(x):
    return pl.pallas_call(
        load_kernel,
        in_specs=[HBM],
        out_specs=VMEM,
        out_shape=jax.ShapeDtypeStruct(x.shape, x.dtype),
        scratch_shapes=[pltpu.SemaphoreType.DMA],
        compiler_params=params(4),
        cost_estimate=cost(0, 2 * x.size),
        name="load_head",
    )(in_hbm(x))


def regroup_kernel(x_ref, o_ref, sem):
    tiles, shards, rows, width = o_ref.shape
    copies = [
        pltpu.make_async_copy(x_ref.at[b, :, pl.ds(k * width, width)], o_ref.at[b, k], sem.at[b, k])
        for b in range(tiles)
        for k in range(shards)
    ]
    for copy in copies:
        copy.start()
    for copy in copies:
        copy.wait()


def regroup(teacher_logits, local_vocab):
    tiles, rows, width = teacher_logits.shape
    shards = width // local_vocab
    return pl.pallas_call(
        regroup_kernel,
        in_specs=[pl.BlockSpec(memory_space=pl.ANY)],
        out_specs=pl.BlockSpec(memory_space=pl.ANY),
        out_shape=jax.ShapeDtypeStruct((tiles, shards, rows, local_vocab), jnp.bfloat16),
        scratch_shapes=[pltpu.SemaphoreType.DMA((tiles, shards))],
        compiler_params=params(4),
        name="teacher_regroup",
    )(teacher_logits)


def teacher_lse_kernel(meta_ref, x_ref, stat_ref, o_ref, acc):
    pairs = x_ref.shape[0] // 16

    def block(i):
        x = x_ref[pl.ds(pl.multiple_of(i * 16, 16), 16), :].astype(jnp.float32)
        return x[:8], x[8:]

    first, second = block(0)
    acc[...] = jnp.maximum(first, second)

    def widen(i, _):
        a, b = block(i)
        acc[...] = jnp.maximum(acc[...], jnp.maximum(a, b))
        return 0

    lax.fori_loop(1, pairs, widen, 0)
    top = jnp.max(acc[...], axis=1, keepdims=True)
    acc[...] = jnp.zeros_like(acc)

    def add(i, _):
        a, b = block(i)
        acc[...] += jnp.exp(a - top) + jnp.exp(b - top)
        return 0

    lax.fori_loop(0, pairs, add, 0)
    lse = top + jnp.log(jnp.sum(acc[...], axis=1, keepdims=True))
    lane = lax.broadcasted_iota(jnp.int32, o_ref.shape, 1)
    row = lax.broadcasted_iota(jnp.int32, o_ref.shape, 0)
    placed = jnp.where(lane == meta_ref[2] * 8 + row, lse, 0.0)
    o_ref[...] = jnp.where(row == 2, jnp.sum(placed, axis=0, keepdims=True), stat_ref[...])


def teacher_lse(rows, meta, stat):
    n, width = rows.shape
    return pl.pallas_call(
        teacher_lse_kernel,
        in_specs=[SMEM, VMEM, VMEM],
        out_specs=VMEM,
        scratch_shapes=[pltpu.VMEM((8, width), jnp.float32)],
        out_shape=jax.ShapeDtypeStruct((8, n), jnp.float32),
        compiler_params=params(4),
        name="teacher_lse",
    )(meta, rows, stat)


ROWS = 32
BLOCK = 512


def column_blocks(width):
    return [(first, min(BLOCK, width - first)) for first in range(0, width, BLOCK)]


def student_kernel(meta_ref, *refs):
    own, other = refs[0:RING], refs[RING : 2 * RING]
    w_ref, s_ref, stat_ref, hidden, logits, sem = refs[2 * RING :]
    rows, width = s_ref.shape
    share = own[0].shape[1]
    core = meta_ref[0]
    for i in range(CHIPS):
        at = slice((i % RING) * rows, (i % RING + 1) * rows)
        chip = meta_ref[3 + i] * 2
        hidden[:, pl.ds(pl.multiple_of((chip + core) * share, share), share)] = own[i // RING][at, :]
        hidden[:, pl.ds(pl.multiple_of((chip + 1 - core) * share, share), share)] = other[i // RING][at, :]
    peaks, totals, copies = [], [], []
    for k, (first, size) in enumerate(column_blocks(width)):
        cols = pl.ds(first, size)
        s = jnp.dot(hidden[...], w_ref[:, cols], preferred_element_type=jnp.float32)
        logits[:, cols] = s
        copies.append(pltpu.make_async_copy(logits.at[:, cols], s_ref.at[:, cols], sem.at[k]))
        copies[k].start()
        peaks.append(jnp.max(s, axis=1, keepdims=True))
        totals.append(jnp.sum(jnp.exp(s - peaks[k]), axis=1, keepdims=True))
    peak = functools.reduce(jnp.maximum, peaks)
    total = functools.reduce(jnp.add, [t * jnp.exp(p - peak) for p, t in zip(peaks, totals)])
    row = lax.broadcasted_iota(jnp.int32, stat_ref.shape, 0)
    stat_ref[...] = jnp.where(row == 0, to_row(peak), jnp.where(row == 1, to_row(total), 0.0))
    for copy in copies:
        copy.wait()


def student_logits(meta, own, other, head_weight):
    depth, width = head_weight.shape
    rows = own[0].shape[0] // RING
    return pl.pallas_call(
        student_kernel,
        in_specs=[SMEM] + [VMEM] * (2 * RING + 1),
        out_specs=[HBM, VMEM],
        out_shape=[
            pltpu.HBM((rows, width), jnp.float32),
            jax.ShapeDtypeStruct((8, rows), jnp.float32),
        ],
        scratch_shapes=[
            pltpu.VMEM((rows, depth), jnp.bfloat16),
            pltpu.VMEM((rows, width), jnp.float32),
            pltpu.SemaphoreType.DMA((len(column_blocks(width)),)),
        ],
        compiler_params=params(12),
        cost_estimate=cost(2 * rows * depth * width, 2 * depth * width),
        name="student_logits",
    )(meta, *own, *other, in_vmem(head_weight))


def ring_sum(parts):
    return (parts[0] + parts[3]) + (parts[1] + parts[2]) if len(parts) == RING else parts[0] + parts[1]


def merged(blocks):
    top = functools.reduce(jnp.maximum, [x[0:1] for x in blocks])
    total = ring_sum([x[1:2] * jnp.exp(x[0:1] - top) for x in blocks])
    return top, total, ring_sum([x[2:3] for x in blocks])


def merge_kernel(*refs):
    o_ref = refs[-1]
    top, total, lse = merged([x[...] for x in refs[:-1]])
    row = lax.broadcasted_iota(jnp.int32, o_ref.shape, 0)
    o_ref[...] = jnp.where(row == 0, top, jnp.where(row == 1, total, lse))


def merge(*blocks):
    return pl.pallas_call(
        merge_kernel,
        out_shape=jax.ShapeDtypeStruct(blocks[0].shape, jnp.float32),
        compiler_params=params(4),
        name="merge_stats",
    )(*blocks)


def split_bf16(x):
    high = x.astype(jnp.bfloat16).astype(jnp.float32)
    rest = x - high
    middle = rest.astype(jnp.bfloat16).astype(jnp.float32)
    return high, middle, rest - middle


CHIP_BLOCK = 4


def share_matmul(w_ref, grad_ref, part_ref):
    chips, share, width = w_ref.shape
    for i in range(0, chips, CHIP_BLOCK):
        out = lax.dot_general(
            w_ref[i : i + CHIP_BLOCK].reshape(CHIP_BLOCK * share, width),
            grad_ref[...],
            (((1,), (1,)), ((), ())),
            preferred_element_type=jnp.float32,
        )
        part_ref[i : i + CHIP_BLOCK] = out.astype(jnp.bfloat16).reshape(CHIP_BLOCK, share, out.shape[1])


def grad_kernel(meta_ref, *refs):
    stats = refs[0:RING]
    s_ref, t_ref, id_ref, weight_ref, w_ref = refs[RING : RING + 5]
    grad_ref, part_ref, tail_ref, own_w_ref, column, cross, picked, logits, head, s_sem, w_sem, own_sem = refs[RING + 5 :]
    rows, width = s_ref.shape
    chips, share, _ = part_ref.shape
    heads = w_ref.reshape(chips, 2, share, width)
    s_copy = pltpu.make_async_copy(s_ref, logits, s_sem)
    w_copy = pltpu.make_async_copy(heads.at[:, 1 - meta_ref[0]], head, w_sem)
    own_copy = pltpu.make_async_copy(heads.at[:, meta_ref[0]], own_w_ref, own_sem)
    s_copy.start()

    top, sums, teacher_row = merged([x[...] for x in stats])
    column[:, 0:1] = to_column(top + jnp.log(sums))
    column[:, 1:2] = to_column(teacher_row)
    column[:, 2:3] = to_column(weight_ref[...])
    column[:, 3:4] = to_column(id_ref[...].astype(jnp.float32))
    lane = lax.broadcasted_iota(jnp.int32, (ROWS, 128), 1)
    s_copy.wait()
    w_copy.start()

    def chunk(i, _):
        at = pl.ds(pl.multiple_of(i * ROWS, ROWS), ROWS)
        student_lse, teacher_lse, weight = column[at, 0:1], column[at, 1:2], column[at, 2:3]
        target = column[at, 3:4].astype(jnp.int32) - meta_ref[1]
        gap = jnp.zeros((ROWS, 128), jnp.float32)
        pick = jnp.zeros((ROWS, 128), jnp.float32)
        for j in range(0, width, 128):
            cols = slice(j, j + 128)
            student_logp = logits[at, cols] - student_lse
            teacher_logp = t_ref[at, cols].astype(jnp.float32) - teacher_lse
            student_prob = jnp.exp(student_logp)
            teacher_prob = jnp.exp(teacher_logp)
            hit = lane == target - j
            onehot = jnp.where(hit, 1.0, 0.0)
            gap += teacher_prob * (teacher_logp - student_logp)
            pick += jnp.where(hit, -student_logp, 0.0)
            grad = weight * ((student_prob - teacher_prob) + CE_WEIGHT * (student_prob - onehot))
            grad_ref[at, cols] = grad.astype(jnp.bfloat16)
        cross[at, :] = gap
        picked[at, :] = pick
        return 0

    lax.fori_loop(0, rows // ROWS, chunk, 0)
    w_copy.wait()
    own_copy.start()
    share_matmul(head, grad_ref, part_ref)

    gap = to_row(jnp.sum(cross[...], axis=1, keepdims=True))
    pick = to_row(jnp.sum(picked[...], axis=1, keepdims=True))
    row = lax.broadcasted_iota(jnp.int32, tail_ref.shape, 0)
    tail = jnp.zeros(tail_ref.shape, jnp.float32)
    for k, line in enumerate(split_bf16(gap) + split_bf16(pick)):
        tail = jnp.where(row == k, line, tail)
    tail_ref[...] = tail.astype(jnp.bfloat16)
    own_copy.wait()


def logit_grad(meta, stats, student, teacher, ids, weights, head_weight):
    depth, width = head_weight.shape
    share = depth // CHIPS // 2
    rows = student.shape[0]
    return pl.pallas_call(
        grad_kernel,
        in_specs=[SMEM] + [VMEM] * RING + [HBM] + [VMEM] * 3 + [HBM],
        out_specs=[VMEM] * 4,
        out_shape=[
            jax.ShapeDtypeStruct((rows, width), jnp.bfloat16),
            jax.ShapeDtypeStruct((CHIPS, share, rows), jnp.bfloat16),
            jax.ShapeDtypeStruct((TAIL, rows), jnp.bfloat16),
            jax.ShapeDtypeStruct((CHIPS, share, width), jnp.bfloat16),
        ],
        scratch_shapes=[
            pltpu.VMEM((rows, 128), jnp.float32),
            pltpu.VMEM((rows, 128), jnp.float32),
            pltpu.VMEM((rows, 128), jnp.float32),
            pltpu.VMEM((rows, width), jnp.float32),
            pltpu.VMEM((CHIPS, share, width), jnp.bfloat16),
            pltpu.SemaphoreType.DMA,
            pltpu.SemaphoreType.DMA,
            pltpu.SemaphoreType.DMA,
        ],
        compiler_params=params(20),
        cost_estimate=cost(rows * depth * width, 2 * depth * width),
        name="logit_grad",
    )(meta, *stats, in_hbm(student), teacher, ids, weights, in_hbm(head_weight))


def own_kernel(grad_ref, w_ref, part_ref):
    share_matmul(w_ref, grad_ref, part_ref)


def own_share(grad, own_w):
    chips, share, width = own_w.shape
    rows = grad.shape[0]
    return pl.pallas_call(
        own_kernel,
        in_specs=[VMEM, VMEM],
        out_specs=VMEM,
        out_shape=jax.ShapeDtypeStruct((chips, share, rows), jnp.bfloat16),
        compiler_params=params(6),
        cost_estimate=cost(2 * rows * chips * share * width, 2 * chips * share * width),
        name="own_share",
    )(grad, in_vmem(own_w))


def join_kernel(a_ref, b_ref, ta_ref, tb_ref, o_ref):
    share = a_ref.shape[1]
    total = a_ref[...].astype(jnp.float32) + b_ref[...].astype(jnp.float32)
    o_ref[:, 0:share, :] = total.astype(jnp.bfloat16)
    tail = jnp.concatenate(
        [ta_ref[...].astype(jnp.float32)[0 : TAIL // 2], tb_ref[...].astype(jnp.float32)[0 : TAIL // 2]]
    ).astype(jnp.bfloat16)
    for i in range(o_ref.shape[0]):
        o_ref[i, share : share + TAIL, :] = tail


def join(a, b, tail_a, tail_b):
    chips, share, rows = a.shape
    block = pl.BlockSpec((CHIP_BLOCK, share, rows), lambda i: (i, 0, 0))
    tail = pl.BlockSpec((TAIL, rows), lambda i: (0, 0))
    return pl.pallas_call(
        join_kernel,
        grid=(chips // CHIP_BLOCK,),
        in_specs=[block, block, tail, tail],
        out_specs=pl.BlockSpec((CHIP_BLOCK, share + TAIL, rows), lambda i: (i, 0, 0)),
        out_shape=jax.ShapeDtypeStruct((chips, share + TAIL, rows), jnp.bfloat16),
        compiler_params=params(16),
        name="chip_sum",
    )(a, b, tail_a, tail_b)


def final_kernel(x_ref, div_ref, ce_ref, o_ref):
    chips = x_ref.shape[0]
    share = x_ref.shape[1] - TAIL
    total = x_ref[0, 0:share, :].astype(jnp.float32)
    for i in range(1, chips):
        total += x_ref[i, 0:share, :].astype(jnp.float32)
    o_ref[...] = total.astype(jnp.bfloat16)
    div = jnp.zeros(div_ref.shape, jnp.float32)
    ce = jnp.zeros(ce_ref.shape, jnp.float32)
    for i in range(chips):
        tail = x_ref[i, share : share + TAIL, :].astype(jnp.float32)
        line = lambda k: tail[k : k + 1]
        value = lambda k: (line(k) + line(k + 1)) + line(k + 2)
        half = TAIL // 2
        div += value(0) + value(half)
        ce += value(3) + value(half + 3)
    div_ref[...] = div
    ce_ref[...] = ce


def final(blocks):
    chips, height, rows = blocks.shape
    return pl.pallas_call(
        final_kernel,
        out_shape=[
            jax.ShapeDtypeStruct((1, rows), jnp.float32),
            jax.ShapeDtypeStruct((1, rows), jnp.float32),
            jax.ShapeDtypeStruct((height - TAIL, rows), jnp.bfloat16),
        ],
        compiler_params=params(16),
        name="final_sum",
    )(blocks)


def on_device(hidden, head_weight, teacher_logits, token_ids, token_weight):
    rows, share = hidden.shape
    depth, width = head_weight.shape
    me = lax.axis_index("vocab")
    core, chip = me % 2, me // 2
    y, z = chip // RING, chip % RING
    sources = [((y - dy) % RING) * RING + (z - dz) % RING for dy in SHIFTS for dz in SHIFTS]

    meta = jnp.stack([core, me * width, me] + sources).astype(jnp.int32)

    along_z = jnp.concatenate(from_ring(hidden, "dz"), axis=0)
    own = from_ring(along_z, "dy")
    blocks = jnp.transpose(after(teacher_logits, along_z, meta), (1, 0, 2))
    blocks = regroup(blocks, width).reshape(rows, width)
    head = load(after(head_weight, blocks))
    blocks = lax.all_to_all(blocks, "tok", 0, 0, tiled=True)
    other = [swap_core(x) for x in own]
    student, stat = student_logits(meta, own, other, head)

    blocks = after(blocks, stat)
    teacher = lax.all_to_all(blocks, "vocab", 0, 0, tiled=True)
    stat = teacher_lse(blocks, meta, stat)
    stat = merge(stat, swap_core(stat))
    stats = from_ring(merge(*from_ring(stat, "dz")), "dy")

    grad, part, tail, own_w = logit_grad(
        meta, stats, student, teacher, token_ids.reshape(1, rows), token_weight.reshape(1, rows), head_weight
    )
    from_core, from_tail = swap_core(part), swap_core(tail)
    mine = own_share(grad, own_w)
    summed = join(mine, from_core, tail, from_tail)

    same_core = [[member(i // RING, i % RING, c) for i in range(CHIPS)] for c in range(2)]
    blocks = lax.all_to_all(
        summed.reshape(CHIPS * (share + TAIL), rows), "vocab", 0, 0, axis_index_groups=same_core, tiled=True
    )
    divergence, cross_entropy, hidden_grad = final(blocks.reshape(CHIPS, share + TAIL, rows))
    return divergence.reshape(rows), cross_entropy.reshape(rows), hidden_grad


def solution(mesh):
    return jax.shard_map(
        on_device,
        mesh=mesh,
        in_specs=(P("tok", "vocab"), P(None, "vocab"), P("vocab", None, "tok"), P("tok"), P("tok")),
        out_specs=(P("tok"), P("tok"), P("vocab", "tok")),
        check_vma=False,
    )
```

```python
import functools

import jax
import jax.numpy as jnp
from jax import lax
from jax.experimental import pallas as pl
from jax.experimental.pallas import tpu as pltpu
from jax.sharding import PartitionSpec as P

CE_WEIGHT = 0.5
RING = 4
CHIPS = RING * RING
SHIFTS = (0, 1, -1, 2)
MIB = 1 << 20
SMEM = pl.BlockSpec(memory_space=pltpu.SMEM)
VMEM = pl.BlockSpec(memory_space=pltpu.VMEM)
HBM = pl.BlockSpec(memory_space=pltpu.HBM)
TAIL = 16


def params(limit):
    return pltpu.CompilerParams(vmem_limit_bytes=limit * MIB)


def cost(flops, read):
    return pl.CostEstimate(flops=flops, bytes_accessed=read, transcendentals=0)


def in_vmem(x):
    return pltpu.with_memory_space_constraint(x, pltpu.VMEM)


def in_hbm(x):
    return pltpu.with_memory_space_constraint(x, pltpu.HBM)


def after(x, *others):
    return lax.optimization_barrier((x,) + others)[0]


def member(y, z, core):
    return ((y % RING) * RING + z % RING) * 2 + core % 2


def moves(dy=0, dz=0, dcore=0):
    return [
        (member(y, z, c), member(y + dy, z + dz, c + dcore))
        for y in range(RING)
        for z in range(RING)
        for c in range(2)
    ]


def swap_core(x):
    return lax.ppermute(x, "vocab", moves(dcore=1))


def from_ring(x, axis):
    return [x] + [lax.ppermute(x, "vocab", moves(**{axis: d})) for d in SHIFTS[1:]]


def eye(n):
    return lax.broadcasted_iota(jnp.int32, (n, n), 0) == lax.broadcasted_iota(jnp.int32, (n, n), 1)


def to_column(row):
    n = row.shape[1]
    return jnp.sum(jnp.where(eye(n), row, 0.0), axis=1, keepdims=True)


def to_row(column):
    n = column.shape[0]
    return jnp.sum(jnp.where(eye(n), column, 0.0), axis=0, keepdims=True)


def regroup_kernel(x_ref, o_ref, sem):
    tiles, shards, rows, width = o_ref.shape
    copies = [
        pltpu.make_async_copy(x_ref.at[b, :, pl.ds(k * width, width)], o_ref.at[b, k], sem.at[b, k])
        for b in range(tiles)
        for k in range(shards)
    ]
    for copy in copies:
        copy.start()
    for copy in copies:
        copy.wait()


def regroup(teacher_logits, local_vocab):
    tiles, rows, width = teacher_logits.shape
    shards = width // local_vocab
    return pl.pallas_call(
        regroup_kernel,
        in_specs=[pl.BlockSpec(memory_space=pl.ANY)],
        out_specs=pl.BlockSpec(memory_space=pl.ANY),
        out_shape=jax.ShapeDtypeStruct((tiles, shards, rows, local_vocab), jnp.bfloat16),
        scratch_shapes=[pltpu.SemaphoreType.DMA((tiles, shards))],
        compiler_params=params(4),
        name="teacher_regroup",
    )(teacher_logits)


ROWS = 32
BLOCK = 512
AHEAD = 2


def column_blocks(width):
    return [(first, min(BLOCK, width - first)) for first in range(0, width, BLOCK)]


def halves(width):
    last = column_blocks(width)[-1][0]
    return [pl.ds(0, last), pl.ds(last, width - last)]


def student_kernel(meta_ref, *refs):
    own, other = refs[0:RING], refs[RING : 2 * RING]
    w_ref, t_ref, s_ref, stat_ref, hidden, logits, peaks, totals, t_peaks, t_totals, head_sem, sem, *heads = refs[2 * RING :]
    rows, width = s_ref.shape
    share = own[0].shape[1]
    core = meta_ref[0]
    blocks = [pl.ds(first, size) for first, size in column_blocks(width)]
    copies = [
        pltpu.make_async_copy(w_ref.at[:, cols], heads[k], head_sem.at[k]) for k, cols in enumerate(blocks)
    ]
    for copy in copies[:AHEAD]:
        copy.start()
    for i in range(CHIPS):
        at = slice((i % RING) * rows, (i % RING + 1) * rows)
        chip = meta_ref[3 + i] * 2
        hidden[:, pl.ds(pl.multiple_of((chip + core) * share, share), share)] = own[i // RING][at, :]
        hidden[:, pl.ds(pl.multiple_of((chip + 1 - core) * share, share), share)] = other[i // RING][at, :]
    outs = [
        pltpu.make_async_copy(logits.at[:, cols], s_ref.at[:, cols], sem.at[k]) for k, cols in enumerate(halves(width))
    ]

    def add(tiles, peak_ref, total_ref, k):
        peak = functools.reduce(jnp.maximum, tiles)
        if k > 0:
            old = peak_ref[...]
            peak = jnp.maximum(peak, old)
        total = functools.reduce(jnp.add, [jnp.exp(x - peak) for x in tiles])
        total_ref[...] = total if k == 0 else total + total_ref[...] * jnp.exp(old - peak)
        peak_ref[...] = peak

    def tally(k):
        first, size = column_blocks(width)[k]
        add([logits[:, j : j + 128] for j in range(first, first + size, 128)], peaks, totals, k)

    def tally_teacher(k):
        first, size = column_blocks(width)[k]
        tiles = []
        for j in range(first, first + size, 128):
            x = t_ref[:, j : j + 128].astype(jnp.float32).reshape(rows // 8, 8, 128)
            tiles += [x[i] for i in range(rows // 8)]
        add(tiles, t_peaks, t_totals, k)

    def across(peak_ref, total_ref):
        peak = jnp.max(peak_ref[...], axis=1, keepdims=True)
        return peak, jnp.sum(total_ref[...] * jnp.exp(peak_ref[...] - peak), axis=1, keepdims=True)

    for k, cols in enumerate(blocks):
        copies[k].wait()
        if k + AHEAD < len(blocks):
            copies[k + AHEAD].start()
        if k + 1 == len(blocks):
            outs[0].start()

        @pl.when(core >= 0)
        def _():
            logits[:, cols] = jnp.dot(hidden[...], heads[k][...], preferred_element_type=jnp.float32)
            tally_teacher(k)
            if k > 0:
                tally(k - 1)

    outs[1].start()
    tally(len(blocks) - 1)
    peak, total = across(peaks, totals)
    t_peak, t_total = across(t_peaks, t_totals)
    row = lax.broadcasted_iota(jnp.int32, stat_ref.shape, 0)
    lane = lax.broadcasted_iota(jnp.int32, stat_ref.shape, 1)
    lse = jnp.where(lane == meta_ref[2] * 8 + row, t_peak + jnp.log(t_total), 0.0)
    lse = jnp.sum(lse, axis=0, keepdims=True)
    stat_ref[...] = jnp.where(row == 0, to_row(peak), jnp.where(row == 1, to_row(total), lse))
    for out in outs:
        out.wait()


def student_logits(meta, own, other, head_weight, teacher_rows):
    depth, width = head_weight.shape
    rows = own[0].shape[0] // RING
    return pl.pallas_call(
        student_kernel,
        in_specs=[SMEM] + [VMEM] * (2 * RING) + [HBM, VMEM],
        out_specs=[HBM, VMEM],
        out_shape=[
            pltpu.HBM((rows, width), jnp.float32),
            jax.ShapeDtypeStruct((8, rows), jnp.float32),
        ],
        scratch_shapes=[
            pltpu.VMEM((rows, depth), jnp.bfloat16),
            pltpu.VMEM((rows, width), jnp.float32),
            pltpu.VMEM((rows, 128), jnp.float32),
            pltpu.VMEM((rows, 128), jnp.float32),
            pltpu.VMEM((8, 128), jnp.float32),
            pltpu.VMEM((8, 128), jnp.float32),
            pltpu.SemaphoreType.DMA((len(column_blocks(width)),)),
            pltpu.SemaphoreType.DMA((2,)),
        ]
        + [pltpu.VMEM((depth, size), jnp.bfloat16) for _, size in column_blocks(width)],
        compiler_params=params(36),
        cost_estimate=cost(2 * rows * depth * width, 2 * depth * width),
        name="student_logits",
    )(meta, *own, *other, in_hbm(head_weight), teacher_rows)


def ring_sum(parts):
    return (parts[0] + parts[3]) + (parts[1] + parts[2]) if len(parts) == RING else parts[0] + parts[1]


def merged(blocks):
    top = functools.reduce(jnp.maximum, [x[0:1] for x in blocks])
    total = ring_sum([x[1:2] * jnp.exp(x[0:1] - top) for x in blocks])
    return top, total, ring_sum([x[2:3] for x in blocks])


def merge_kernel(*refs):
    o_ref = refs[-1]
    top, total, lse = merged([x[...] for x in refs[:-1]])
    row = lax.broadcasted_iota(jnp.int32, o_ref.shape, 0)
    o_ref[...] = jnp.where(row == 0, top, jnp.where(row == 1, total, lse))


def merge(*blocks):
    return pl.pallas_call(
        merge_kernel,
        out_shape=jax.ShapeDtypeStruct(blocks[0].shape, jnp.float32),
        compiler_params=params(4),
        name="merge_stats",
    )(*blocks)


def split_bf16(x):
    high = x.astype(jnp.bfloat16).astype(jnp.float32)
    rest = x - high
    middle = rest.astype(jnp.bfloat16).astype(jnp.float32)
    return high, middle, rest - middle


CHIP_BLOCK = 4
SECOND = 5


def share_matmul(w_ref, grad_ref, part_ref):
    chips, share, width = w_ref.shape
    for i in range(0, chips, CHIP_BLOCK):
        out = lax.dot_general(
            w_ref[i : i + CHIP_BLOCK].reshape(CHIP_BLOCK * share, width),
            grad_ref[...],
            (((1,), (1,)), ((), ())),
            preferred_element_type=jnp.float32,
        )
        part_ref[i : i + CHIP_BLOCK] = out.astype(jnp.bfloat16).reshape(CHIP_BLOCK, share, out.shape[1])


def grad_kernel(meta_ref, *refs):
    stats = refs[0:RING]
    s_ref, t_ref, id_ref, weight_ref, w_ref = refs[RING : RING + 5]
    grad_ref, part_ref, tail_ref, own_w_ref, column, cross, picked, logits, head, s_sem, w_sem, own_sem = refs[RING + 5 :]
    rows, width = s_ref.shape
    chips, share, _ = part_ref.shape
    heads = w_ref.reshape(chips, 2, share, width)
    s_copy = pltpu.make_async_copy(s_ref, logits, s_sem)
    w_copy = pltpu.make_async_copy(heads.at[:, 1 - meta_ref[0]], head, w_sem)
    own_copy = pltpu.make_async_copy(heads.at[:, meta_ref[0]], own_w_ref, own_sem)
    s_copy.start()
    w_copy.start()

    top, sums, teacher_row = merged([x[...] for x in stats])
    column[:, 0:1] = to_column(top + jnp.log(sums))
    column[:, 1:2] = to_column(teacher_row)
    column[:, 2:3] = to_column(weight_ref[...])
    column[:, 3:4] = to_column(id_ref[...].astype(jnp.float32))
    lane = lax.broadcasted_iota(jnp.int32, (ROWS, 128), 1)
    s_copy.wait()

    def chunk(i, _):
        at = pl.ds(pl.multiple_of(i * ROWS, ROWS), ROWS)
        student_lse, teacher_lse, weight = column[at, 0:1], column[at, 1:2], column[at, 2:3]
        target = column[at, 3:4].astype(jnp.int32) - meta_ref[1]
        gap = jnp.zeros((ROWS, 128), jnp.float32)
        pick = jnp.zeros((ROWS, 128), jnp.float32)
        for j in range(0, width, 128):
            cols = slice(j, j + 128)
            student_logp = logits[at, cols] - student_lse
            teacher_logp = t_ref[at, cols].astype(jnp.float32) - teacher_lse
            student_prob = jnp.exp(student_logp)
            teacher_prob = jnp.exp(teacher_logp)
            hit = lane == target - j
            onehot = jnp.where(hit, 1.0, 0.0)
            gap += teacher_prob * (teacher_logp - student_logp)
            pick += jnp.where(hit, -student_logp, 0.0)
            grad = weight * ((student_prob - teacher_prob) + CE_WEIGHT * (student_prob - onehot))
            grad_ref[at, cols] = grad.astype(jnp.bfloat16)
        cross[at, :] = gap
        picked[at, :] = pick

        @pl.when(i == SECOND)
        def _():
            w_copy.wait()
            own_copy.start()

        return 0

    lax.fori_loop(0, rows // ROWS, chunk, 0)
    share_matmul(head, grad_ref, part_ref)

    gap = to_row(jnp.sum(cross[...], axis=1, keepdims=True))
    pick = to_row(jnp.sum(picked[...], axis=1, keepdims=True))
    row = lax.broadcasted_iota(jnp.int32, tail_ref.shape, 0)
    tail = jnp.zeros(tail_ref.shape, jnp.float32)
    for k, line in enumerate(split_bf16(gap) + split_bf16(pick)):
        tail = jnp.where(row == k, line, tail)
    tail_ref[...] = tail.astype(jnp.bfloat16)
    own_copy.wait()


def logit_grad(meta, stats, student, teacher, ids, weights, head_weight):
    depth, width = head_weight.shape
    share = depth // CHIPS // 2
    rows = student.shape[0]
    return pl.pallas_call(
        grad_kernel,
        in_specs=[SMEM] + [VMEM] * RING + [HBM] + [VMEM] * 3 + [HBM],
        out_specs=[VMEM] * 4,
        out_shape=[
            jax.ShapeDtypeStruct((rows, width), jnp.bfloat16),
            jax.ShapeDtypeStruct((CHIPS, share, rows), jnp.bfloat16),
            jax.ShapeDtypeStruct((TAIL, rows), jnp.bfloat16),
            jax.ShapeDtypeStruct((CHIPS, share, width), jnp.bfloat16),
        ],
        scratch_shapes=[
            pltpu.VMEM((rows, 128), jnp.float32),
            pltpu.VMEM((rows, 128), jnp.float32),
            pltpu.VMEM((rows, 128), jnp.float32),
            pltpu.VMEM((rows, width), jnp.float32),
            pltpu.VMEM((CHIPS, share, width), jnp.bfloat16),
            pltpu.SemaphoreType.DMA,
            pltpu.SemaphoreType.DMA,
            pltpu.SemaphoreType.DMA,
        ],
        compiler_params=params(20),
        cost_estimate=cost(rows * depth * width, 2 * depth * width),
        name="logit_grad",
    )(meta, *stats, in_hbm(student), teacher, ids, weights, in_hbm(head_weight))


def own_kernel(grad_ref, w_ref, part_ref):
    share_matmul(w_ref, grad_ref, part_ref)


def own_share(grad, own_w):
    chips, share, width = own_w.shape
    rows = grad.shape[0]
    return pl.pallas_call(
        own_kernel,
        in_specs=[VMEM, VMEM],
        out_specs=VMEM,
        out_shape=jax.ShapeDtypeStruct((chips, share, rows), jnp.bfloat16),
        compiler_params=params(6),
        cost_estimate=cost(2 * rows * chips * share * width, 2 * chips * share * width),
        name="own_share",
    )(grad, in_vmem(own_w))


def join_kernel(a_ref, b_ref, ta_ref, tb_ref, o_ref):
    share = a_ref.shape[1]
    total = a_ref[...].astype(jnp.float32) + b_ref[...].astype(jnp.float32)
    o_ref[:, 0:share, :] = total.astype(jnp.bfloat16)
    tail = jnp.concatenate(
        [ta_ref[...].astype(jnp.float32)[0 : TAIL // 2], tb_ref[...].astype(jnp.float32)[0 : TAIL // 2]]
    ).astype(jnp.bfloat16)
    for i in range(o_ref.shape[0]):
        o_ref[i, share : share + TAIL, :] = tail


def join(a, b, tail_a, tail_b):
    chips, share, rows = a.shape
    block = pl.BlockSpec((CHIP_BLOCK, share, rows), lambda i: (i, 0, 0))
    tail = pl.BlockSpec((TAIL, rows), lambda i: (0, 0))
    return pl.pallas_call(
        join_kernel,
        grid=(chips // CHIP_BLOCK,),
        in_specs=[block, block, tail, tail],
        out_specs=pl.BlockSpec((CHIP_BLOCK, share + TAIL, rows), lambda i: (i, 0, 0)),
        out_shape=jax.ShapeDtypeStruct((chips, share + TAIL, rows), jnp.bfloat16),
        compiler_params=params(16),
        name="chip_sum",
    )(a, b, tail_a, tail_b)


def final_kernel(x_ref, div_ref, ce_ref, o_ref):
    chips = x_ref.shape[0]
    share = x_ref.shape[1] - TAIL
    total = x_ref[0, 0:share, :].astype(jnp.float32)
    for i in range(1, chips):
        total += x_ref[i, 0:share, :].astype(jnp.float32)
    o_ref[...] = total.astype(jnp.bfloat16)
    div = jnp.zeros(div_ref.shape, jnp.float32)
    ce = jnp.zeros(ce_ref.shape, jnp.float32)
    for i in range(chips):
        tail = x_ref[i, share : share + TAIL, :].astype(jnp.float32)
        line = lambda k: tail[k : k + 1]
        value = lambda k: (line(k) + line(k + 1)) + line(k + 2)
        half = TAIL // 2
        div += value(0) + value(half)
        ce += value(3) + value(half + 3)
    div_ref[...] = div
    ce_ref[...] = ce


def final(blocks):
    chips, height, rows = blocks.shape
    return pl.pallas_call(
        final_kernel,
        out_shape=[
            jax.ShapeDtypeStruct((1, rows), jnp.float32),
            jax.ShapeDtypeStruct((1, rows), jnp.float32),
            jax.ShapeDtypeStruct((height - TAIL, rows), jnp.bfloat16),
        ],
        compiler_params=params(16),
        name="final_sum",
    )(blocks)


def on_device(hidden, head_weight, teacher_logits, token_ids, token_weight):
    rows, share = hidden.shape
    depth, width = head_weight.shape
    me = lax.axis_index("vocab")
    core, chip = me % 2, me // 2
    y, z = chip // RING, chip % RING
    sources = [((y - dy) % RING) * RING + (z - dz) % RING for dy in SHIFTS for dz in SHIFTS]

    meta = jnp.stack([core, me * width, me] + sources).astype(jnp.int32)

    along_z = jnp.concatenate(from_ring(hidden, "dz"), axis=0)
    blocks = jnp.transpose(teacher_logits, (1, 0, 2)).reshape(rows // 8, -1)
    blocks = lax.all_to_all(after(blocks, along_z, meta), "tok", 0, 0, tiled=True)
    own = from_ring(along_z, "dy")
    blocks = regroup(blocks.reshape(-1, 8, blocks.shape[1]), width).reshape(rows, width)

    other = [swap_core(x) for x in own]
    blocks = after(blocks, *other)
    teacher = lax.all_to_all(blocks, "vocab", 0, 0, tiled=True)
    student, stat = student_logits(meta, own, other, head_weight, blocks)
    stat = merge(stat, swap_core(stat))
    stats = from_ring(merge(*from_ring(stat, "dz")), "dy")

    grad, part, tail, own_w = logit_grad(
        meta, stats, student, teacher, token_ids.reshape(1, rows), token_weight.reshape(1, rows), head_weight
    )
    from_core, from_tail = swap_core(part), swap_core(tail)
    mine = own_share(grad, own_w)
    summed = join(mine, from_core, tail, from_tail)

    same_core = [[member(i // RING, i % RING, c) for i in range(CHIPS)] for c in range(2)]
    blocks = lax.all_to_all(
        summed.reshape(CHIPS * (share + TAIL), rows), "vocab", 0, 0, axis_index_groups=same_core, tiled=True
    )
    divergence, cross_entropy, hidden_grad = final(blocks.reshape(CHIPS, share + TAIL, rows))
    return divergence.reshape(rows), cross_entropy.reshape(rows), hidden_grad


def solution(mesh):
    return jax.shard_map(
        on_device,
        mesh=mesh,
        in_specs=(P("tok", "vocab"), P(None, "vocab"), P("vocab", None, "tok"), P("tok"), P("tok")),
        out_specs=(P("tok"), P("tok"), P("vocab", "tok")),
        check_vma=False,
    )
```

```python
import functools

import jax
import jax.numpy as jnp
from jax import lax
from jax.experimental import pallas as pl
from jax.experimental.pallas import tpu as pltpu
from jax.sharding import PartitionSpec as P

CE_WEIGHT = 0.5
RING = 4
CHIPS = RING * RING
SHIFTS = (0, 1, -1, 2)
MIB = 1 << 20
SMEM = pl.BlockSpec(memory_space=pltpu.SMEM)
VMEM = pl.BlockSpec(memory_space=pltpu.VMEM)
HBM = pl.BlockSpec(memory_space=pltpu.HBM)
TAIL = 16


def params(limit):
    return pltpu.CompilerParams(vmem_limit_bytes=limit * MIB)


def cost(flops, read):
    return pl.CostEstimate(flops=flops, bytes_accessed=read, transcendentals=0)


def in_vmem(x):
    return pltpu.with_memory_space_constraint(x, pltpu.VMEM)


def in_hbm(x):
    return pltpu.with_memory_space_constraint(x, pltpu.HBM)


def after(x, *others):
    return lax.optimization_barrier((x,) + others)[0]


def member(y, z, core):
    return ((y % RING) * RING + z % RING) * 2 + core % 2


def moves(dy=0, dz=0, dcore=0):
    return [
        (member(y, z, c), member(y + dy, z + dz, c + dcore))
        for y in range(RING)
        for z in range(RING)
        for c in range(2)
    ]


def swap_core(x):
    return lax.ppermute(x, "vocab", moves(dcore=1))


def from_ring(x, axis):
    return [x] + [lax.ppermute(x, "vocab", moves(**{axis: d})) for d in SHIFTS[1:]]


def eye(n):
    return lax.broadcasted_iota(jnp.int32, (n, n), 0) == lax.broadcasted_iota(jnp.int32, (n, n), 1)


def to_column(row):
    n = row.shape[1]
    return jnp.sum(jnp.where(eye(n), row, 0.0), axis=1, keepdims=True)


def to_row(column):
    n = column.shape[0]
    return jnp.sum(jnp.where(eye(n), column, 0.0), axis=0, keepdims=True)


ROWS = 32
BLOCK = 512
AHEAD = 2


def column_blocks(width):
    return [(first, min(BLOCK, width - first)) for first in range(0, width, BLOCK)]


def parts_of(x, count):
    parts = []
    for _ in range(count):
        parts.append(x.astype(jnp.bfloat16).astype(jnp.float32))
        x = x - parts[-1]
    return parts


def student_kernel(meta_ref, *refs):
    blocks = column_blocks(refs[2 * RING + 2].shape[1])
    n = len(blocks)
    own, other = refs[0:RING], refs[RING : 2 * RING]
    w_ref, x_ref, s_ref, send_ref = refs[2 * RING : 2 * RING + 4]
    heads = refs[2 * RING + 4 : 2 * RING + 4 + n]
    hidden, peaks, totals, t_peaks, t_totals, sem = refs[2 * RING + 4 + n :]
    rows, width = s_ref.shape
    tiles_x, shards = x_ref.shape[0], x_ref.shape[2] // width
    share = own[0].shape[1]
    core = meta_ref[0]
    copies = [
        pltpu.make_async_copy(w_ref.at[:, pl.ds(first, size)], heads[k], sem.at[k])
        for k, (first, size) in enumerate(blocks)
    ]
    for copy in copies[:AHEAD]:
        copy.start()
    for i in range(CHIPS):
        at = slice((i % RING) * rows, (i % RING + 1) * rows)
        chip = meta_ref[3 + i] * 2
        hidden[:, pl.ds(pl.multiple_of((chip + core) * share, share), share)] = own[i // RING][at, :]
        hidden[:, pl.ds(pl.multiple_of((chip + 1 - core) * share, share), share)] = other[i // RING][at, :]

    def add(tiles, peak_ref, total_ref, k):
        peak = functools.reduce(jnp.maximum, tiles)
        if k > 0:
            old = peak_ref[...]
            peak = jnp.maximum(peak, old)
        total = functools.reduce(jnp.add, [jnp.exp(x - peak) for x in tiles])
        total_ref[...] = total if k == 0 else total + total_ref[...] * jnp.exp(old - peak)
        peak_ref[...] = peak

    def tally(k):
        first, size = blocks[k]
        add([s_ref[:, j : j + 128] for j in range(first, first + size, 128)], peaks, totals, k)

    def tally_teacher(k):
        first, size = blocks[k]
        tiles = []
        for i in range(tiles_x):
            for j in range(shards):
                x = x_ref[i, :, j * width + first : j * width + first + size]
                send_ref[i * shards + j, :, first : first + size] = x
                x = x.astype(jnp.float32)
                tiles += [x[:, c : c + 128] for c in range(0, size, 128)]
        add(tiles, t_peaks, t_totals, k)

    for k, (first, size) in enumerate(blocks):
        copies[k].wait()
        if k + AHEAD < n:
            copies[k + AHEAD].start()

        @pl.when(core >= 0)
        def _():
            s_ref[:, first : first + size] = jnp.dot(
                hidden[...], heads[k][...], preferred_element_type=jnp.float32
            )
            tally_teacher(k)
            if k > 0:
                tally(k - 1)

    tally(n - 1)
    peak = parts_of(jnp.max(peaks[...], axis=1, keepdims=True), 2)
    total = jnp.sum(totals[...] * jnp.exp(peaks[...] - (peak[0] + peak[1])), axis=1, keepdims=True)
    t_peak = jnp.max(t_peaks[...], axis=1, keepdims=True)
    t_total = jnp.sum(t_totals[...] * jnp.exp(t_peaks[...] - t_peak), axis=1, keepdims=True)
    row = lax.broadcasted_iota(jnp.int32, (8, rows), 0)
    lane = lax.broadcasted_iota(jnp.int32, (8, rows), 1)
    lse = jnp.where(lane == meta_ref[2] * 8 + row, t_peak + jnp.log(t_total), 0.0)
    lse = jnp.sum(lse, axis=0, keepdims=True)
    lines = [to_row(x) for x in peak] + parts_of(to_row(total), 3) + parts_of(lse, 3)
    stat = jnp.zeros((8, rows), jnp.float32)
    for k, line in enumerate(lines):
        stat = jnp.where(row == k, line, stat)
    stat = stat.astype(jnp.bfloat16)
    for i in range(send_ref.shape[0]):
        send_ref[i, :, width:] = stat


def student_logits(meta, own, other, head_weight, teacher_rows):
    depth, width = head_weight.shape
    rows = own[0].shape[0] // RING
    blocks = column_blocks(width)
    return pl.pallas_call(
        student_kernel,
        in_specs=[SMEM] + [VMEM] * (2 * RING) + [HBM, VMEM],
        out_specs=[VMEM] * (2 + len(blocks)),
        out_shape=[
            jax.ShapeDtypeStruct((rows, width), jnp.float32),
            jax.ShapeDtypeStruct((2 * CHIPS, 8, width + rows), jnp.bfloat16),
        ]
        + [jax.ShapeDtypeStruct((depth, size), jnp.bfloat16) for _, size in blocks],
        scratch_shapes=[
            pltpu.VMEM((rows, depth), jnp.bfloat16),
            pltpu.VMEM((rows, 128), jnp.float32),
            pltpu.VMEM((rows, 128), jnp.float32),
            pltpu.VMEM((8, 128), jnp.float32),
            pltpu.VMEM((8, 128), jnp.float32),
            pltpu.SemaphoreType.DMA((len(blocks),)),
        ],
        compiler_params=params(10),
        cost_estimate=cost(2 * rows * depth * width, 2 * depth * width),
        name="student_logits",
    )(meta, *own, *other, in_hbm(head_weight), teacher_rows)


def merged(stats):
    peaks = [x[0:1] + x[1:2] for x in stats]
    top = functools.reduce(jnp.maximum, peaks)
    total = functools.reduce(
        jnp.add, [((x[2:3] + x[3:4]) + x[4:5]) * jnp.exp(p - top) for x, p in zip(stats, peaks)]
    )
    return top + jnp.log(total), functools.reduce(jnp.add, [(x[5:6] + x[6:7]) + x[7:8] for x in stats])


def head_rows(head, core, chips):
    depth, size = head.shape
    share = depth // CHIPS // 2
    return head.reshape(CHIPS, 2, share, size)[chips, core].reshape(-1, size)


def grad_kernel(meta_ref, x_ref, s_ref, id_ref, weight_ref, *refs):
    blocks = column_blocks(s_ref.shape[1])
    heads = refs[: len(blocks)]
    grad_ref, part_ref, tail_ref, column, cross, picked, total = refs[len(blocks) :]
    rows, width = s_ref.shape
    stats = [x_ref[i, :, width:].astype(jnp.float32) for i in range(x_ref.shape[0])]
    student_row, teacher_row = merged(stats)
    column[:, 0:1] = to_column(student_row)
    column[:, 1:2] = to_column(teacher_row)
    column[:, 2:3] = to_column(weight_ref[...])
    column[:, 3:4] = to_column(id_ref[...].astype(jnp.float32))
    lane = lax.broadcasted_iota(jnp.int32, (ROWS, 128), 1)

    for k, (first, size) in enumerate(blocks):
        for r in range(0, rows, ROWS):
            at = slice(r, r + ROWS)
            student_lse, teacher_lse, weight = column[at, 0:1], column[at, 1:2], column[at, 2:3]
            target = column[at, 3:4].astype(jnp.int32) - meta_ref[1]
            gap = jnp.zeros((ROWS, 128), jnp.float32) if k == 0 else cross[at, :]
            pick = jnp.zeros((ROWS, 128), jnp.float32) if k == 0 else picked[at, :]
            for j in range(first, first + size, 128):
                cols = slice(j, j + 128)
                student_logp = s_ref[at, cols] - student_lse
                teacher = x_ref[r // 8 : (r + ROWS) // 8, :, cols].astype(jnp.float32).reshape(ROWS, 128)
                teacher_logp = teacher - teacher_lse
                student_prob = jnp.exp(student_logp)
                teacher_prob = jnp.exp(teacher_logp)
                hit = lane == target - j
                onehot = jnp.where(hit, 1.0, 0.0)
                gap += teacher_prob * (teacher_logp - student_logp)
                pick += jnp.where(hit, -student_logp, 0.0)
                grad = weight * ((student_prob - teacher_prob) + CE_WEIGHT * (student_prob - onehot))
                grad_ref[at, cols] = grad.astype(jnp.bfloat16)
            cross[at, :] = gap
            picked[at, :] = pick
        out = lax.dot_general(
            head_rows(heads[k], 1 - meta_ref[0], slice(0, CHIPS)),
            grad_ref[:, first : first + size],
            (((1,), (1,)), ((), ())),
            preferred_element_type=jnp.float32,
        )
        if k == 0:
            total[...] = out
        elif k + 1 < len(blocks):
            total[...] += out
        else:
            part_ref[...] = (total[...] + out).astype(jnp.bfloat16).reshape(part_ref.shape)

    gap = to_row(jnp.sum(cross[...], axis=1, keepdims=True))
    pick = to_row(jnp.sum(picked[...], axis=1, keepdims=True))
    row = lax.broadcasted_iota(jnp.int32, tail_ref.shape, 0)
    tail = jnp.zeros(tail_ref.shape, jnp.float32)
    for k, line in enumerate(parts_of(gap, 3) + parts_of(pick, 3)):
        tail = jnp.where(row == k, line, tail)
    tail_ref[...] = tail.astype(jnp.bfloat16)


def logit_grad(meta, teacher, student, ids, weights, heads):
    rows, width = student.shape
    depth = heads[0].shape[0]
    share = depth // CHIPS // 2
    return pl.pallas_call(
        grad_kernel,
        in_specs=[SMEM] + [VMEM] * (4 + len(heads)),
        out_specs=[VMEM] * 3,
        out_shape=[
            jax.ShapeDtypeStruct((rows, width), jnp.bfloat16),
            jax.ShapeDtypeStruct((CHIPS, share, rows), jnp.bfloat16),
            jax.ShapeDtypeStruct((TAIL, rows), jnp.bfloat16),
        ],
        scratch_shapes=[
            pltpu.VMEM((rows, 128), jnp.float32),
            pltpu.VMEM((rows, 128), jnp.float32),
            pltpu.VMEM((rows, 128), jnp.float32),
            pltpu.VMEM((CHIPS * share, rows), jnp.float32),
        ],
        compiler_params=params(14),
        cost_estimate=cost(rows * depth * width, depth * width),
        name="logit_grad",
    )(meta, teacher, student, ids, weights, *[in_vmem(x) for x in heads])


CHIP_BLOCK = 4


def own_kernel(meta_ref, grad_ref, *refs):
    heads, part_ref = refs[:-1], refs[-1]
    chips, share, rows = part_ref.shape
    for i in range(0, chips, CHIP_BLOCK):
        total = 0.0
        for k, (first, size) in enumerate(column_blocks(grad_ref.shape[1])):
            total += lax.dot_general(
                head_rows(heads[k], meta_ref[0], slice(i, i + CHIP_BLOCK)),
                grad_ref[:, first : first + size],
                (((1,), (1,)), ((), ())),
                preferred_element_type=jnp.float32,
            )
        part_ref[i : i + CHIP_BLOCK] = total.astype(jnp.bfloat16).reshape(CHIP_BLOCK, share, rows)


def own_share(meta, grad, heads):
    rows, width = grad.shape
    depth = heads[0].shape[0]
    share = depth // CHIPS // 2
    return pl.pallas_call(
        own_kernel,
        in_specs=[SMEM] + [VMEM] * (1 + len(heads)),
        out_specs=VMEM,
        out_shape=jax.ShapeDtypeStruct((CHIPS, share, rows), jnp.bfloat16),
        compiler_params=params(8),
        cost_estimate=cost(rows * depth * width, depth * width),
        name="own_share",
    )(meta, grad, *[in_vmem(x) for x in heads])


def join_kernel(a_ref, b_ref, ta_ref, tb_ref, o_ref):
    share = a_ref.shape[1]
    total = a_ref[...].astype(jnp.float32) + b_ref[...].astype(jnp.float32)
    o_ref[:, 0:share, :] = total.astype(jnp.bfloat16)
    tail = jnp.concatenate(
        [ta_ref[...].astype(jnp.float32)[0 : TAIL // 2], tb_ref[...].astype(jnp.float32)[0 : TAIL // 2]]
    ).astype(jnp.bfloat16)
    for i in range(o_ref.shape[0]):
        o_ref[i, share : share + TAIL, :] = tail


def join(a, b, tail_a, tail_b):
    chips, share, rows = a.shape
    block = pl.BlockSpec((CHIP_BLOCK, share, rows), lambda i: (i, 0, 0))
    tail = pl.BlockSpec((TAIL, rows), lambda i: (0, 0))
    return pl.pallas_call(
        join_kernel,
        grid=(chips // CHIP_BLOCK,),
        in_specs=[block, block, tail, tail],
        out_specs=pl.BlockSpec((CHIP_BLOCK, share + TAIL, rows), lambda i: (i, 0, 0)),
        out_shape=jax.ShapeDtypeStruct((chips, share + TAIL, rows), jnp.bfloat16),
        compiler_params=params(16),
        name="chip_sum",
    )(a, b, tail_a, tail_b)


def final_kernel(x_ref, div_ref, ce_ref, o_ref):
    chips = x_ref.shape[0]
    share = x_ref.shape[1] - TAIL
    total = x_ref[0, 0:share, :].astype(jnp.float32)
    for i in range(1, chips):
        total += x_ref[i, 0:share, :].astype(jnp.float32)
    o_ref[...] = total.astype(jnp.bfloat16)
    div = jnp.zeros(div_ref.shape, jnp.float32)
    ce = jnp.zeros(ce_ref.shape, jnp.float32)
    for i in range(chips):
        tail = x_ref[i, share : share + TAIL, :].astype(jnp.float32)
        line = lambda k: tail[k : k + 1]
        value = lambda k: (line(k) + line(k + 1)) + line(k + 2)
        half = TAIL // 2
        div += value(0) + value(half)
        ce += value(3) + value(half + 3)
    div_ref[...] = div
    ce_ref[...] = ce


def final(blocks):
    chips, height, rows = blocks.shape
    return pl.pallas_call(
        final_kernel,
        out_shape=[
            jax.ShapeDtypeStruct((1, rows), jnp.float32),
            jax.ShapeDtypeStruct((1, rows), jnp.float32),
            jax.ShapeDtypeStruct((height - TAIL, rows), jnp.bfloat16),
        ],
        compiler_params=params(16),
        name="final_sum",
    )(blocks)


def on_device(hidden, head_weight, teacher_logits, token_ids, token_weight):
    rows, share = hidden.shape
    depth, width = head_weight.shape
    me = lax.axis_index("vocab")
    core, chip = me % 2, me // 2
    y, z = chip // RING, chip % RING
    sources = [((y - dy) % RING) * RING + (z - dz) % RING for dy in SHIFTS for dz in SHIFTS]

    meta = jnp.stack([core, me * width, me] + sources).astype(jnp.int32)

    along_z = jnp.concatenate(from_ring(hidden, "dz"), axis=0)
    blocks = jnp.transpose(teacher_logits, (1, 0, 2)).reshape(rows // 8, -1)
    blocks = lax.all_to_all(after(blocks, along_z, meta), "tok", 0, 0, tiled=True)
    own = from_ring(along_z, "dy")
    other = [swap_core(x) for x in own]
    student, send, *heads = student_logits(
        meta, own, other, head_weight, blocks.reshape(-1, 8, blocks.shape[1])
    )

    teacher = lax.all_to_all(send, "vocab", 0, 0, tiled=True)
    grad, part, tail = logit_grad(
        meta, teacher, student, token_ids.reshape(1, rows), token_weight.reshape(1, rows), heads
    )
    from_core, from_tail = swap_core(part), swap_core(tail)
    mine = own_share(meta, grad, heads)
    summed = join(mine, from_core, tail, from_tail)

    same_core = [[member(i // RING, i % RING, c) for i in range(CHIPS)] for c in range(2)]
    blocks = lax.all_to_all(
        summed.reshape(CHIPS * (share + TAIL), rows), "vocab", 0, 0, axis_index_groups=same_core, tiled=True
    )
    divergence, cross_entropy, hidden_grad = final(blocks.reshape(CHIPS, share + TAIL, rows))
    return divergence.reshape(rows), cross_entropy.reshape(rows), hidden_grad


def solution(mesh):
    return jax.shard_map(
        on_device,
        mesh=mesh,
        in_specs=(P("tok", "vocab"), P(None, "vocab"), P("vocab", None, "tok"), P("tok"), P("tok")),
        out_specs=(P("tok"), P("tok"), P("vocab", "tok")),
        check_vma=False,
    )
```

```python
import functools

import jax
import jax.numpy as jnp
from jax import lax
from jax.experimental import pallas as pl
from jax.experimental.pallas import tpu as pltpu
from jax.sharding import PartitionSpec as P

CE_WEIGHT = 0.5
RING = 4
CHIPS = RING * RING
SHIFTS = (0, 1, -1, 2)
MIB = 1 << 20
SMEM = pl.BlockSpec(memory_space=pltpu.SMEM)
VMEM = pl.BlockSpec(memory_space=pltpu.VMEM)
HBM = pl.BlockSpec(memory_space=pltpu.HBM)
TAIL = 16


def params(limit):
    return pltpu.CompilerParams(vmem_limit_bytes=limit * MIB)


def cost(flops, read):
    return pl.CostEstimate(flops=flops, bytes_accessed=read, transcendentals=0)


def in_vmem(x):
    return pltpu.with_memory_space_constraint(x, pltpu.VMEM)


def in_hbm(x):
    return pltpu.with_memory_space_constraint(x, pltpu.HBM)


def after(x, *others):
    return lax.optimization_barrier((x,) + others)[0]


def member(y, z, core):
    return ((y % RING) * RING + z % RING) * 2 + core % 2


def moves(dy=0, dz=0, dcore=0):
    return [
        (member(y, z, c), member(y + dy, z + dz, c + dcore))
        for y in range(RING)
        for z in range(RING)
        for c in range(2)
    ]


def swap_core(x):
    return lax.ppermute(x, "vocab", moves(dcore=1))


def from_ring(x, axis):
    return [x] + [lax.ppermute(x, "vocab", moves(**{axis: d})) for d in SHIFTS[1:]]


def eye(n):
    return lax.broadcasted_iota(jnp.int32, (n, n), 0) == lax.broadcasted_iota(jnp.int32, (n, n), 1)


def to_column(row):
    n = row.shape[1]
    return jnp.sum(jnp.where(eye(n), row, 0.0), axis=1, keepdims=True)


def to_row(column):
    n = column.shape[0]
    return jnp.sum(jnp.where(eye(n), column, 0.0), axis=0, keepdims=True)


ROWS = 32
BLOCK = 512
AHEAD = 2


def column_blocks(width):
    return [(first, min(BLOCK, width - first)) for first in range(0, width, BLOCK)]


def parts_of(x, count):
    parts = []
    for _ in range(count):
        parts.append(x.astype(jnp.bfloat16).astype(jnp.float32))
        x = x - parts[-1]
    return parts


def student_kernel(meta_ref, *refs):
    blocks = column_blocks(refs[2 * RING + 2].shape[1])
    n = len(blocks)
    own, other = refs[0:RING], refs[RING : 2 * RING]
    w_ref, x_ref, s_ref, send_ref = refs[2 * RING : 2 * RING + 4]
    heads = refs[2 * RING + 4 : 2 * RING + 4 + n]
    hidden, peaks, totals, t_peaks, t_totals, sem = refs[2 * RING + 4 + n :]
    rows, width = s_ref.shape
    tiles_x, shards = x_ref.shape[0], x_ref.shape[2] // width
    share = own[0].shape[1]
    core = meta_ref[0]
    copies = [
        pltpu.make_async_copy(w_ref.at[:, pl.ds(first, size)], heads[k], sem.at[k])
        for k, (first, size) in enumerate(blocks)
    ]
    for copy in copies[:AHEAD]:
        copy.start()
    for i in range(CHIPS):
        at = slice((i % RING) * rows, (i % RING + 1) * rows)
        chip = meta_ref[3 + i] * 2
        hidden[:, pl.ds(pl.multiple_of((chip + core) * share, share), share)] = own[i // RING][at, :]
        hidden[:, pl.ds(pl.multiple_of((chip + 1 - core) * share, share), share)] = other[i // RING][at, :]

    def add(tiles, peak_ref, total_ref, k):
        peak = functools.reduce(jnp.maximum, tiles)
        if k > 0:
            old = peak_ref[...]
            peak = jnp.maximum(peak, old)
        total = functools.reduce(jnp.add, [jnp.exp(x - peak) for x in tiles])
        total_ref[...] = total if k == 0 else total + total_ref[...] * jnp.exp(old - peak)
        peak_ref[...] = peak

    def tally(k):
        first, size = blocks[k]
        add([s_ref[:, j : j + 128] for j in range(first, first + size, 128)], peaks, totals, k)

    def tally_teacher(k):
        first, size = blocks[k]
        tiles = []
        for i in range(tiles_x):
            for j in range(shards):
                x = x_ref[i, :, j * width + first : j * width + first + size]
                send_ref[i * shards + j, :, first : first + size] = x
                x = x.astype(jnp.float32)
                tiles += [x[:, c : c + 128] for c in range(0, size, 128)]
        add(tiles, t_peaks, t_totals, k)

    for k, (first, size) in enumerate(blocks):
        copies[k].wait()
        if k + AHEAD < n:
            copies[k + AHEAD].start()

        @pl.when(core >= 0)
        def _():
            s_ref[:, first : first + size] = jnp.dot(
                hidden[...], heads[k][...], preferred_element_type=jnp.float32
            )
            tally_teacher(k)
            if k > 0:
                tally(k - 1)

    tally(n - 1)
    peak = parts_of(jnp.max(peaks[...], axis=1, keepdims=True), 2)
    total = jnp.sum(totals[...] * jnp.exp(peaks[...] - (peak[0] + peak[1])), axis=1, keepdims=True)
    t_peak = jnp.max(t_peaks[...], axis=1, keepdims=True)
    t_total = jnp.sum(t_totals[...] * jnp.exp(t_peaks[...] - t_peak), axis=1, keepdims=True)
    row = lax.broadcasted_iota(jnp.int32, (8, rows), 0)
    lane = lax.broadcasted_iota(jnp.int32, (8, rows), 1)
    lse = jnp.where(lane == meta_ref[2] * 8 + row, t_peak + jnp.log(t_total), 0.0)
    lse = jnp.sum(lse, axis=0, keepdims=True)
    lines = [to_row(x) for x in peak] + parts_of(to_row(total), 3) + parts_of(lse, 3)
    stat = jnp.zeros((8, rows), jnp.float32)
    for k, line in enumerate(lines):
        stat = jnp.where(row == k, line, stat)
    stat = stat.astype(jnp.bfloat16)
    for i in range(send_ref.shape[0]):
        send_ref[i, :, width:] = stat


def student_logits(meta, own, other, head_weight, teacher_rows):
    depth, width = head_weight.shape
    rows = own[0].shape[0] // RING
    blocks = column_blocks(width)
    return pl.pallas_call(
        student_kernel,
        in_specs=[SMEM] + [VMEM] * (2 * RING) + [HBM, VMEM],
        out_specs=[VMEM] * (2 + len(blocks)),
        out_shape=[
            jax.ShapeDtypeStruct((rows, width), jnp.float32),
            jax.ShapeDtypeStruct((2 * CHIPS, 8, width + rows), jnp.bfloat16),
        ]
        + [jax.ShapeDtypeStruct((depth, size), jnp.bfloat16) for _, size in blocks],
        scratch_shapes=[
            pltpu.VMEM((rows, depth), jnp.bfloat16),
            pltpu.VMEM((rows, 128), jnp.float32),
            pltpu.VMEM((rows, 128), jnp.float32),
            pltpu.VMEM((8, 128), jnp.float32),
            pltpu.VMEM((8, 128), jnp.float32),
            pltpu.SemaphoreType.DMA((len(blocks),)),
        ],
        compiler_params=params(10),
        cost_estimate=cost(2 * rows * depth * width, 2 * depth * width),
        name="student_logits",
    )(meta, *own, *other, in_hbm(head_weight), teacher_rows)


def merged(stats):
    peaks = [x[0:1] + x[1:2] for x in stats]
    top = functools.reduce(jnp.maximum, peaks)
    total = functools.reduce(
        jnp.add, [((x[2:3] + x[3:4]) + x[4:5]) * jnp.exp(p - top) for x, p in zip(stats, peaks)]
    )
    return top + jnp.log(total), functools.reduce(jnp.add, [(x[5:6] + x[6:7]) + x[7:8] for x in stats])


def head_rows(head, core, chips):
    depth, size = head.shape
    share = depth // CHIPS // 2
    return head.reshape(CHIPS, 2, share, size)[chips, core].reshape(-1, size)


def grad_kernel(meta_ref, x_ref, s_ref, id_ref, weight_ref, *refs):
    blocks = column_blocks(s_ref.shape[1])
    heads = refs[: len(blocks)]
    grad_ref, part_ref, tail_ref, column, cross, picked, total = refs[len(blocks) :]
    rows, width = s_ref.shape
    stats = [x_ref[i, :, width:].astype(jnp.float32) for i in range(x_ref.shape[0])]
    student_row, teacher_row = merged(stats)
    column[:, 0:1] = to_column(student_row)
    column[:, 1:2] = to_column(teacher_row)
    column[:, 2:3] = to_column(weight_ref[...])
    column[:, 3:4] = to_column(id_ref[...].astype(jnp.float32))
    lane = lax.broadcasted_iota(jnp.int32, (ROWS, 128), 1)

    for k, (first, size) in enumerate(blocks):
        for r in range(0, rows, ROWS):
            at = slice(r, r + ROWS)
            student_lse, teacher_lse, weight = column[at, 0:1], column[at, 1:2], column[at, 2:3]
            target = column[at, 3:4].astype(jnp.int32) - meta_ref[1]
            gap = jnp.zeros((ROWS, 128), jnp.float32) if k == 0 else cross[at, :]
            pick = jnp.zeros((ROWS, 128), jnp.float32) if k == 0 else picked[at, :]
            for j in range(first, first + size, 128):
                cols = slice(j, j + 128)
                student_logp = s_ref[at, cols] - student_lse
                teacher = x_ref[r // 8 : (r + ROWS) // 8, :, cols].astype(jnp.float32).reshape(ROWS, 128)
                teacher_logp = teacher - teacher_lse
                student_prob = jnp.exp(student_logp)
                teacher_prob = jnp.exp(teacher_logp)
                hit = lane == target - j
                onehot = jnp.where(hit, 1.0, 0.0)
                gap += teacher_prob * (teacher_logp - student_logp)
                pick += jnp.where(hit, -student_logp, 0.0)
                grad = weight * ((student_prob - teacher_prob) + CE_WEIGHT * (student_prob - onehot))
                grad_ref[at, cols] = grad.astype(jnp.bfloat16)
            cross[at, :] = gap
            picked[at, :] = pick
        out = lax.dot_general(
            head_rows(heads[k], 1 - meta_ref[0], slice(0, CHIPS)),
            grad_ref[:, first : first + size],
            (((1,), (1,)), ((), ())),
            preferred_element_type=jnp.float32,
        )
        if k == 0:
            total[...] = out
        elif k + 1 < len(blocks):
            total[...] += out
        else:
            part_ref[...] = (total[...] + out).astype(jnp.bfloat16).reshape(part_ref.shape)

    gap = to_row(jnp.sum(cross[...], axis=1, keepdims=True))
    pick = to_row(jnp.sum(picked[...], axis=1, keepdims=True))
    row = lax.broadcasted_iota(jnp.int32, tail_ref.shape, 0)
    tail = jnp.zeros(tail_ref.shape, jnp.float32)
    for k, line in enumerate(parts_of(gap, 3) + parts_of(pick, 3)):
        tail = jnp.where(row == k, line, tail)
    tail_ref[...] = tail.astype(jnp.bfloat16)


def logit_grad(meta, teacher, student, ids, weights, heads):
    rows, width = student.shape
    depth = heads[0].shape[0]
    share = depth // CHIPS // 2
    return pl.pallas_call(
        grad_kernel,
        in_specs=[SMEM] + [VMEM] * (4 + len(heads)),
        out_specs=[VMEM] * 3,
        out_shape=[
            jax.ShapeDtypeStruct((rows, width), jnp.bfloat16),
            jax.ShapeDtypeStruct((CHIPS, share, rows), jnp.bfloat16),
            jax.ShapeDtypeStruct((TAIL, rows), jnp.bfloat16),
        ],
        scratch_shapes=[
            pltpu.VMEM((rows, 128), jnp.float32),
            pltpu.VMEM((rows, 128), jnp.float32),
            pltpu.VMEM((rows, 128), jnp.float32),
            pltpu.VMEM((CHIPS * share, rows), jnp.float32),
        ],
        compiler_params=params(14),
        cost_estimate=cost(rows * depth * width, depth * width),
        name="logit_grad",
    )(meta, teacher, student, ids, weights, *[in_vmem(x) for x in heads])


CHIP_BLOCK = 4


def own_kernel(meta_ref, grad_ref, *refs):
    heads, part_ref = refs[:-1], refs[-1]
    chips, share, rows = part_ref.shape
    for i in range(0, chips, CHIP_BLOCK):
        total = 0.0
        for k, (first, size) in enumerate(column_blocks(grad_ref.shape[1])):
            total += lax.dot_general(
                head_rows(heads[k], meta_ref[0], slice(i, i + CHIP_BLOCK)),
                grad_ref[:, first : first + size],
                (((1,), (1,)), ((), ())),
                preferred_element_type=jnp.float32,
            )
        part_ref[i : i + CHIP_BLOCK] = total.astype(jnp.bfloat16).reshape(CHIP_BLOCK, share, rows)


def own_share(meta, grad, heads):
    rows, width = grad.shape
    depth = heads[0].shape[0]
    share = depth // CHIPS // 2
    return pl.pallas_call(
        own_kernel,
        in_specs=[SMEM] + [VMEM] * (1 + len(heads)),
        out_specs=VMEM,
        out_shape=jax.ShapeDtypeStruct((CHIPS, share, rows), jnp.bfloat16),
        compiler_params=params(8),
        cost_estimate=cost(rows * depth * width, depth * width),
        name="own_share",
    )(meta, grad, *[in_vmem(x) for x in heads])


def join_kernel(a_ref, b_ref, ta_ref, tb_ref, o_ref):
    share = a_ref.shape[1]
    total = a_ref[...].astype(jnp.float32) + b_ref[...].astype(jnp.float32)
    o_ref[:, 0:share, :] = total.astype(jnp.bfloat16)
    tail = jnp.concatenate(
        [ta_ref[...].astype(jnp.float32)[0 : TAIL // 2], tb_ref[...].astype(jnp.float32)[0 : TAIL // 2]]
    ).astype(jnp.bfloat16)
    for i in range(o_ref.shape[0]):
        o_ref[i, share : share + TAIL, :] = tail


def join(a, b, tail_a, tail_b):
    chips, share, rows = a.shape
    block = pl.BlockSpec((CHIP_BLOCK, share, rows), lambda i: (i, 0, 0))
    tail = pl.BlockSpec((TAIL, rows), lambda i: (0, 0))
    return pl.pallas_call(
        join_kernel,
        grid=(chips // CHIP_BLOCK,),
        in_specs=[block, block, tail, tail],
        out_specs=pl.BlockSpec((CHIP_BLOCK, share + TAIL, rows), lambda i: (i, 0, 0)),
        out_shape=jax.ShapeDtypeStruct((chips, share + TAIL, rows), jnp.bfloat16),
        compiler_params=params(16),
        name="chip_sum",
    )(a, b, tail_a, tail_b)


def final_kernel(x_ref, div_ref, ce_ref, o_ref):
    chips = x_ref.shape[0]
    share = x_ref.shape[1] - TAIL
    total = x_ref[0, 0:share, :].astype(jnp.float32)
    for i in range(1, chips):
        total += x_ref[i, 0:share, :].astype(jnp.float32)
    o_ref[...] = total.astype(jnp.bfloat16)
    div = jnp.zeros(div_ref.shape, jnp.float32)
    ce = jnp.zeros(ce_ref.shape, jnp.float32)
    for i in range(chips):
        tail = x_ref[i, share : share + TAIL, :].astype(jnp.float32)
        line = lambda k: tail[k : k + 1]
        value = lambda k: (line(k) + line(k + 1)) + line(k + 2)
        half = TAIL // 2
        div += value(0) + value(half)
        ce += value(3) + value(half + 3)
    div_ref[...] = div
    ce_ref[...] = ce


def final(blocks):
    chips, height, rows = blocks.shape
    return pl.pallas_call(
        final_kernel,
        out_shape=[
            jax.ShapeDtypeStruct((1, rows), jnp.float32),
            jax.ShapeDtypeStruct((1, rows), jnp.float32),
            jax.ShapeDtypeStruct((height - TAIL, rows), jnp.bfloat16),
        ],
        compiler_params=params(16),
        name="final_sum",
    )(blocks)


def on_device(hidden, head_weight, teacher_logits, token_ids, token_weight):
    rows, share = hidden.shape
    depth, width = head_weight.shape
    me = lax.axis_index("vocab")
    core, chip = me % 2, me // 2
    y, z = chip // RING, chip % RING
    sources = [((y - dy) % RING) * RING + (z - dz) % RING for dy in SHIFTS for dz in SHIFTS]

    meta = jnp.stack([core, me * width, me] + sources).astype(jnp.int32)

    along_z = jnp.concatenate(from_ring(hidden, "dz"), axis=0)
    blocks = jnp.transpose(teacher_logits, (1, 0, 2)).reshape(rows // 8, -1)
    blocks = lax.all_to_all(after(blocks, meta), "tok", 0, 0, tiled=True)
    own = from_ring(along_z, "dy")
    other = [swap_core(x) for x in own]
    student, send, *heads = student_logits(
        meta, own, other, head_weight, blocks.reshape(-1, 8, blocks.shape[1])
    )

    teacher = lax.all_to_all(send, "vocab", 0, 0, tiled=True)
    grad, part, tail = logit_grad(
        meta, teacher, student, token_ids.reshape(1, rows), token_weight.reshape(1, rows), heads
    )
    from_core, from_tail = swap_core(part), swap_core(tail)
    mine = own_share(meta, grad, heads)
    summed = join(mine, from_core, tail, from_tail)

    same_core = [[member(i // RING, i % RING, c) for i in range(CHIPS)] for c in range(2)]
    blocks = lax.all_to_all(
        summed.reshape(CHIPS * (share + TAIL), rows), "vocab", 0, 0, axis_index_groups=same_core, tiled=True
    )
    divergence, cross_entropy, hidden_grad = final(blocks.reshape(CHIPS, share + TAIL, rows))
    return divergence.reshape(rows), cross_entropy.reshape(rows), hidden_grad


def solution(mesh):
    return jax.shard_map(
        on_device,
        mesh=mesh,
        in_specs=(P("tok", "vocab"), P(None, "vocab"), P("vocab", None, "tok"), P("tok"), P("tok")),
        out_specs=(P("tok"), P("tok"), P("vocab", "tok")),
        check_vma=False,
    )
```

```python
import functools

import jax
import jax.numpy as jnp
from jax import lax
from jax.experimental import pallas as pl
from jax.experimental.pallas import tpu as pltpu
from jax.sharding import PartitionSpec as P

CE_WEIGHT = 0.5
RING = 4
CHIPS = RING * RING
SHIFTS = (0, 1, -1, 2)
MIB = 1 << 20
SMEM = pl.BlockSpec(memory_space=pltpu.SMEM)
VMEM = pl.BlockSpec(memory_space=pltpu.VMEM)
HBM = pl.BlockSpec(memory_space=pltpu.HBM)
TAIL = 16


def params(limit):
    return pltpu.CompilerParams(vmem_limit_bytes=limit * MIB)


def cost(flops, read):
    return pl.CostEstimate(flops=flops, bytes_accessed=read, transcendentals=0)


def in_vmem(x):
    return pltpu.with_memory_space_constraint(x, pltpu.VMEM)


def in_hbm(x):
    return pltpu.with_memory_space_constraint(x, pltpu.HBM)


def after(x, *others):
    return lax.optimization_barrier((x,) + others)[0]


def member(y, z, core):
    return ((y % RING) * RING + z % RING) * 2 + core % 2


def moves(dy=0, dz=0, dcore=0):
    return [
        (member(y, z, c), member(y + dy, z + dz, c + dcore))
        for y in range(RING)
        for z in range(RING)
        for c in range(2)
    ]


def swap_core(x):
    return lax.ppermute(x, "vocab", moves(dcore=1))


def from_ring(x, axis):
    return [x] + [lax.ppermute(x, "vocab", moves(**{axis: d})) for d in SHIFTS[1:]]


def eye(n):
    return lax.broadcasted_iota(jnp.int32, (n, n), 0) == lax.broadcasted_iota(jnp.int32, (n, n), 1)


def to_column(row):
    n = row.shape[1]
    return jnp.sum(jnp.where(eye(n), row, 0.0), axis=1, keepdims=True)


def to_row(column):
    n = column.shape[0]
    return jnp.sum(jnp.where(eye(n), column, 0.0), axis=0, keepdims=True)


ROWS = 32
BLOCK = 512
AHEAD = 2


def column_blocks(width):
    return [(first, min(BLOCK, width - first)) for first in range(0, width, BLOCK)]


def parts_of(x, count):
    parts = []
    for _ in range(count):
        parts.append(x.astype(jnp.bfloat16).astype(jnp.float32))
        x = x - parts[-1]
    return parts


def student_kernel(meta_ref, *refs):
    blocks = column_blocks(refs[2 * RING + 2].shape[1])
    n = len(blocks)
    own, other = refs[0:RING], refs[RING : 2 * RING]
    w_ref, x_ref, s_ref, send_ref = refs[2 * RING : 2 * RING + 4]
    heads = refs[2 * RING + 4 : 2 * RING + 4 + n]
    hidden, peaks, totals, t_peaks, t_totals, sem = refs[2 * RING + 4 + n :]
    rows, width = s_ref.shape
    tiles_x, shards = x_ref.shape[0], x_ref.shape[2] // width
    share = own[0].shape[1]
    core = meta_ref[0]
    copies = [
        pltpu.make_async_copy(w_ref.at[:, pl.ds(first, size)], heads[k], sem.at[k])
        for k, (first, size) in enumerate(blocks)
    ]
    for copy in copies[:AHEAD]:
        copy.start()
    for i in range(CHIPS):
        at = slice((i % RING) * rows, (i % RING + 1) * rows)
        chip = meta_ref[3 + i] * 2
        hidden[:, pl.ds(pl.multiple_of((chip + core) * share, share), share)] = own[i // RING][at, :]
        hidden[:, pl.ds(pl.multiple_of((chip + 1 - core) * share, share), share)] = other[i // RING][at, :]

    def add(tiles, peak_ref, total_ref, k):
        peak = functools.reduce(jnp.maximum, tiles)
        if k > 0:
            old = peak_ref[...]
            peak = jnp.maximum(peak, old)
        total = functools.reduce(jnp.add, [jnp.exp(x - peak) for x in tiles])
        total_ref[...] = total if k == 0 else total + total_ref[...] * jnp.exp(old - peak)
        peak_ref[...] = peak

    def tally(k):
        first, size = blocks[k]
        add([s_ref[:, j : j + 128] for j in range(first, first + size, 128)], peaks, totals, k)

    def tally_teacher(k):
        first, size = blocks[k]
        tiles = []
        for i in range(tiles_x):
            for j in range(shards):
                x = x_ref[i, :, j * width + first : j * width + first + size]
                send_ref[i * shards + j, :, first : first + size] = x
                x = x.astype(jnp.float32)
                tiles += [x[:, c : c + 128] for c in range(0, size, 128)]
        add(tiles, t_peaks, t_totals, k)

    for k, (first, size) in enumerate(blocks):
        copies[k].wait()
        if k + AHEAD < n:
            copies[k + AHEAD].start()

        @pl.when(core >= 0)
        def _():
            s_ref[:, first : first + size] = jnp.dot(
                hidden[...], heads[k][...], preferred_element_type=jnp.float32
            )
            tally_teacher(k)
            if k > 0:
                tally(k - 1)

    tally(n - 1)
    peak = jnp.max(peaks[...], axis=1, keepdims=True)
    lse = peak + jnp.log(jnp.sum(totals[...] * jnp.exp(peaks[...] - peak), axis=1, keepdims=True))
    t_peak = jnp.max(t_peaks[...], axis=1, keepdims=True)
    t_lse = t_peak + jnp.log(jnp.sum(t_totals[...] * jnp.exp(t_peaks[...] - t_peak), axis=1, keepdims=True))
    row = lax.broadcasted_iota(jnp.int32, (8, 128), 0)
    lane = lax.broadcasted_iota(jnp.int32, (8, 128), 1)
    lines = [part[:, h : h + 128] for part in parts_of(to_row(lse), 3) for h in range(0, rows, 128)]
    t_line = jnp.zeros((8, 128), jnp.float32)
    for k, part in enumerate(parts_of(t_lse, 3)):
        t_line = jnp.where(lane == k * 8 + row, part, t_line)
    lines.append(jnp.sum(t_line, axis=0, keepdims=True))
    stat = jnp.zeros((8, 128), jnp.float32)
    for k, line in enumerate(lines):
        stat = jnp.where(row == k, line, stat)
    stat = stat.astype(jnp.bfloat16)
    for i in range(send_ref.shape[0]):
        send_ref[i, :, width:] = stat


def student_logits(meta, own, other, head_weight, teacher_rows):
    depth, width = head_weight.shape
    rows = own[0].shape[0] // RING
    blocks = column_blocks(width)
    return pl.pallas_call(
        student_kernel,
        in_specs=[SMEM] + [VMEM] * (2 * RING) + [HBM, VMEM],
        out_specs=[VMEM] * (2 + len(blocks)),
        out_shape=[
            jax.ShapeDtypeStruct((rows, width), jnp.float32),
            jax.ShapeDtypeStruct((2 * CHIPS, 8, width + 128), jnp.bfloat16),
        ]
        + [jax.ShapeDtypeStruct((depth, size), jnp.bfloat16) for _, size in blocks],
        scratch_shapes=[
            pltpu.VMEM((rows, depth), jnp.bfloat16),
            pltpu.VMEM((rows, 128), jnp.float32),
            pltpu.VMEM((rows, 128), jnp.float32),
            pltpu.VMEM((8, 128), jnp.float32),
            pltpu.VMEM((8, 128), jnp.float32),
            pltpu.SemaphoreType.DMA((len(blocks),)),
        ],
        compiler_params=params(10),
        cost_estimate=cost(2 * rows * depth * width, 2 * depth * width),
        name="student_logits",
    )(meta, *own, *other, in_hbm(head_weight), teacher_rows)


def merged(stats, rows):
    halves = rows // 128
    line = lambda x, k: jnp.concatenate([x[k * halves + h : k * halves + h + 1] for h in range(halves)], axis=1)
    lses = [(line(x, 0) + line(x, 1)) + line(x, 2) for x in stats]
    top = functools.reduce(jnp.maximum, lses)
    total = functools.reduce(jnp.add, [jnp.exp(x - top) for x in lses])
    teacher = jnp.concatenate([x[3 * halves : 3 * halves + 1] for x in stats], axis=0)
    teacher = jnp.broadcast_to(teacher[:, None, :], (len(stats), 8, 128)).reshape(rows, 128)
    row = lax.broadcasted_iota(jnp.int32, (rows, 128), 0)
    lane = lax.broadcasted_iota(jnp.int32, (rows, 128), 1)
    mine = jnp.logical_and(lane < 24, lax.rem(lane, 8) == lax.rem(row, 8))
    return top + jnp.log(total), jnp.sum(jnp.where(mine, teacher, 0.0), axis=1, keepdims=True)


def head_rows(head, core, chips):
    depth, size = head.shape
    share = depth // CHIPS // 2
    return head.reshape(CHIPS, 2, share, size)[chips, core].reshape(-1, size)


def grad_kernel(meta_ref, x_ref, s_ref, id_ref, weight_ref, *refs):
    blocks = column_blocks(s_ref.shape[1])
    heads = refs[: len(blocks)]
    grad_ref, part_ref, tail_ref, column, cross, picked, total = refs[len(blocks) :]
    rows, width = s_ref.shape
    stats = [x_ref[i, :, width:].astype(jnp.float32) for i in range(x_ref.shape[0])]
    student_row, teacher_column = merged(stats, rows)
    column[:, 0:1] = to_column(student_row)
    column[:, 1:2] = teacher_column
    column[:, 2:3] = to_column(weight_ref[...])
    column[:, 3:4] = to_column(id_ref[...].astype(jnp.float32))
    lane = lax.broadcasted_iota(jnp.int32, (ROWS, 128), 1)

    steps = [
        (k, first + low, low, min(STEP, size - low))
        for k, (first, size) in enumerate(blocks)
        for low in range(0, size, STEP)
    ]
    for k, (block, first, low, size) in enumerate(steps):
        for r in range(0, rows, ROWS):
            at = slice(r, r + ROWS)
            student_lse, teacher_lse, weight = column[at, 0:1], column[at, 1:2], column[at, 2:3]
            target = column[at, 3:4].astype(jnp.int32) - meta_ref[1]
            gap = jnp.zeros((ROWS, 128), jnp.float32) if k == 0 else cross[at, :]
            pick = jnp.zeros((ROWS, 128), jnp.float32) if k == 0 else picked[at, :]
            for j in range(first, first + size, 128):
                cols = slice(j, j + 128)
                student_logp = s_ref[at, cols] - student_lse
                teacher = x_ref[r // 8 : (r + ROWS) // 8, :, cols].astype(jnp.float32).reshape(ROWS, 128)
                teacher_logp = teacher - teacher_lse
                student_prob = jnp.exp(student_logp)
                teacher_prob = jnp.exp(teacher_logp)
                hit = lane == target - j
                onehot = jnp.where(hit, 1.0, 0.0)
                gap += teacher_prob * (teacher_logp - student_logp)
                pick += jnp.where(hit, -student_logp, 0.0)
                grad = weight * ((student_prob - teacher_prob) + CE_WEIGHT * (student_prob - onehot))
                grad_ref[at, cols] = grad.astype(jnp.bfloat16)
            cross[at, :] = gap
            picked[at, :] = pick
        out = lax.dot_general(
            head_rows(heads[block], 1 - meta_ref[0], slice(0, CHIPS))[:, low : low + size],
            grad_ref[:, first : first + size],
            (((1,), (1,)), ((), ())),
            preferred_element_type=jnp.float32,
        )
        if k == 0:
            total[...] = out
        elif k + 1 < len(steps):
            total[...] += out
        else:
            part_ref[...] = (total[...] + out).astype(jnp.bfloat16).reshape(part_ref.shape)

    gap = to_row(jnp.sum(cross[...], axis=1, keepdims=True))
    pick = to_row(jnp.sum(picked[...], axis=1, keepdims=True))
    row = lax.broadcasted_iota(jnp.int32, tail_ref.shape, 0)
    tail = jnp.zeros(tail_ref.shape, jnp.float32)
    for k, line in enumerate(parts_of(gap, 3) + parts_of(pick, 3)):
        tail = jnp.where(row == k, line, tail)
    tail_ref[...] = tail.astype(jnp.bfloat16)


def logit_grad(meta, teacher, student, ids, weights, heads):
    rows, width = student.shape
    depth = heads[0].shape[0]
    share = depth // CHIPS // 2
    return pl.pallas_call(
        grad_kernel,
        in_specs=[SMEM] + [VMEM] * (4 + len(heads)),
        out_specs=[VMEM] * 3,
        out_shape=[
            jax.ShapeDtypeStruct((rows, width), jnp.bfloat16),
            jax.ShapeDtypeStruct((CHIPS, share, rows), jnp.bfloat16),
            jax.ShapeDtypeStruct((TAIL, rows), jnp.bfloat16),
        ],
        scratch_shapes=[
            pltpu.VMEM((rows, 128), jnp.float32),
            pltpu.VMEM((rows, 128), jnp.float32),
            pltpu.VMEM((rows, 128), jnp.float32),
            pltpu.VMEM((CHIPS * share, rows), jnp.float32),
        ],
        compiler_params=params(14),
        cost_estimate=cost(rows * depth * width, depth * width),
        name="logit_grad",
    )(meta, teacher, student, ids, weights, *[in_vmem(x) for x in heads])


CHIP_BLOCK = 4
STEP = 256


def own_kernel(meta_ref, grad_ref, *refs):
    heads, part_ref = refs[:-1], refs[-1]
    chips, share, rows = part_ref.shape
    for i in range(0, chips, CHIP_BLOCK):
        total = 0.0
        for k, (first, size) in enumerate(column_blocks(grad_ref.shape[1])):
            total += lax.dot_general(
                head_rows(heads[k], meta_ref[0], slice(i, i + CHIP_BLOCK)),
                grad_ref[:, first : first + size],
                (((1,), (1,)), ((), ())),
                preferred_element_type=jnp.float32,
            )
        part_ref[i : i + CHIP_BLOCK] = total.astype(jnp.bfloat16).reshape(CHIP_BLOCK, share, rows)


def own_share(meta, grad, heads):
    rows, width = grad.shape
    depth = heads[0].shape[0]
    share = depth // CHIPS // 2
    return pl.pallas_call(
        own_kernel,
        in_specs=[SMEM] + [VMEM] * (1 + len(heads)),
        out_specs=VMEM,
        out_shape=jax.ShapeDtypeStruct((CHIPS, share, rows), jnp.bfloat16),
        compiler_params=params(8),
        cost_estimate=cost(rows * depth * width, depth * width),
        name="own_share",
    )(meta, grad, *[in_vmem(x) for x in heads])


def join_kernel(a_ref, b_ref, ta_ref, tb_ref, o_ref):
    share = a_ref.shape[1]
    total = a_ref[...].astype(jnp.float32) + b_ref[...].astype(jnp.float32)
    o_ref[:, 0:share, :] = total.astype(jnp.bfloat16)
    tail = jnp.concatenate(
        [ta_ref[...].astype(jnp.float32)[0 : TAIL // 2], tb_ref[...].astype(jnp.float32)[0 : TAIL // 2]]
    ).astype(jnp.bfloat16)
    for i in range(o_ref.shape[0]):
        o_ref[i, share : share + TAIL, :] = tail


def join(a, b, tail_a, tail_b):
    chips, share, rows = a.shape
    block = pl.BlockSpec((CHIP_BLOCK, share, rows), lambda i: (i, 0, 0))
    tail = pl.BlockSpec((TAIL, rows), lambda i: (0, 0))
    return pl.pallas_call(
        join_kernel,
        grid=(chips // CHIP_BLOCK,),
        in_specs=[block, block, tail, tail],
        out_specs=pl.BlockSpec((CHIP_BLOCK, share + TAIL, rows), lambda i: (i, 0, 0)),
        out_shape=jax.ShapeDtypeStruct((chips, share + TAIL, rows), jnp.bfloat16),
        compiler_params=params(16),
        name="chip_sum",
    )(a, b, tail_a, tail_b)


def final_kernel(x_ref, div_ref, ce_ref, o_ref):
    chips = x_ref.shape[0]
    share = x_ref.shape[1] - TAIL
    total = x_ref[0, 0:share, :].astype(jnp.float32)
    for i in range(1, chips):
        total += x_ref[i, 0:share, :].astype(jnp.float32)
    o_ref[...] = total.astype(jnp.bfloat16)
    div = jnp.zeros(div_ref.shape, jnp.float32)
    ce = jnp.zeros(ce_ref.shape, jnp.float32)
    for i in range(chips):
        tail = x_ref[i, share : share + TAIL, :].astype(jnp.float32)
        line = lambda k: tail[k : k + 1]
        value = lambda k: (line(k) + line(k + 1)) + line(k + 2)
        half = TAIL // 2
        div += value(0) + value(half)
        ce += value(3) + value(half + 3)
    div_ref[...] = div
    ce_ref[...] = ce


def final(blocks):
    chips, height, rows = blocks.shape
    return pl.pallas_call(
        final_kernel,
        out_shape=[
            jax.ShapeDtypeStruct((1, rows), jnp.float32),
            jax.ShapeDtypeStruct((1, rows), jnp.float32),
            jax.ShapeDtypeStruct((height - TAIL, rows), jnp.bfloat16),
        ],
        compiler_params=params(16),
        name="final_sum",
    )(blocks)


def on_device(hidden, head_weight, teacher_logits, token_ids, token_weight):
    rows, share = hidden.shape
    depth, width = head_weight.shape
    me = lax.axis_index("vocab")
    core, chip = me % 2, me // 2
    y, z = chip // RING, chip % RING
    sources = [((y - dy) % RING) * RING + (z - dz) % RING for dy in SHIFTS for dz in SHIFTS]

    meta = jnp.stack([core, me * width, me] + sources).astype(jnp.int32)

    along_z = jnp.concatenate(from_ring(hidden, "dz"), axis=0)
    blocks = jnp.transpose(teacher_logits, (1, 0, 2)).reshape(rows // 8, -1)
    blocks = lax.all_to_all(after(blocks, meta), "tok", 0, 0, tiled=True)
    own = from_ring(along_z, "dy")
    other = [swap_core(x) for x in own]
    student, send, *heads = student_logits(
        meta, own, other, head_weight, blocks.reshape(-1, 8, blocks.shape[1])
    )

    teacher = lax.all_to_all(send, "vocab", 0, 0, tiled=True)
    grad, part, tail = logit_grad(
        meta, teacher, student, token_ids.reshape(1, rows), token_weight.reshape(1, rows), heads
    )
    from_core, from_tail = swap_core(part), swap_core(tail)
    mine = own_share(meta, grad, heads)
    summed = join(mine, from_core, tail, from_tail)

    same_core = [[member(i // RING, i % RING, c) for i in range(CHIPS)] for c in range(2)]
    blocks = lax.all_to_all(
        summed.reshape(CHIPS * (share + TAIL), rows), "vocab", 0, 0, axis_index_groups=same_core, tiled=True
    )
    divergence, cross_entropy, hidden_grad = final(blocks.reshape(CHIPS, share + TAIL, rows))
    return divergence.reshape(rows), cross_entropy.reshape(rows), hidden_grad


def solution(mesh):
    return jax.shard_map(
        on_device,
        mesh=mesh,
        in_specs=(P("tok", "vocab"), P(None, "vocab"), P("vocab", None, "tok"), P("tok"), P("tok")),
        out_specs=(P("tok"), P("tok"), P("vocab", "tok")),
        check_vma=False,
    )
```

```python
import functools

import jax
import jax.numpy as jnp
from jax import lax
from jax.experimental import pallas as pl
from jax.experimental.pallas import tpu as pltpu
from jax.sharding import PartitionSpec as P

CE_WEIGHT = 0.5
RING = 4
CHIPS = RING * RING
SHIFTS = (0, 1, -1, 2)
MIB = 1 << 20
SMEM = pl.BlockSpec(memory_space=pltpu.SMEM)
VMEM = pl.BlockSpec(memory_space=pltpu.VMEM)
HBM = pl.BlockSpec(memory_space=pltpu.HBM)
TAIL = 16


def params(limit):
    return pltpu.CompilerParams(vmem_limit_bytes=limit * MIB)


def cost(flops, read):
    return pl.CostEstimate(flops=flops, bytes_accessed=read, transcendentals=0)


def in_vmem(x):
    return pltpu.with_memory_space_constraint(x, pltpu.VMEM)


def in_hbm(x):
    return pltpu.with_memory_space_constraint(x, pltpu.HBM)


def after(x, *others):
    return lax.optimization_barrier((x,) + others)[0]


def member(y, z, core):
    return ((y % RING) * RING + z % RING) * 2 + core % 2


def moves(dy=0, dz=0, dcore=0):
    return [
        (member(y, z, c), member(y + dy, z + dz, c + dcore))
        for y in range(RING)
        for z in range(RING)
        for c in range(2)
    ]


def swap_core(x):
    return lax.ppermute(x, "vocab", moves(dcore=1))


def from_ring(x, axis):
    return [x] + [lax.ppermute(x, "vocab", moves(**{axis: d})) for d in SHIFTS[1:]]


def eye(n):
    return lax.broadcasted_iota(jnp.int32, (n, n), 0) == lax.broadcasted_iota(jnp.int32, (n, n), 1)


def to_column(row):
    n = row.shape[1]
    return jnp.sum(jnp.where(eye(n), row, 0.0), axis=1, keepdims=True)


def to_row(column):
    n = column.shape[0]
    return jnp.sum(jnp.where(eye(n), column, 0.0), axis=0, keepdims=True)


ROWS = 32
FIRST = 384
BLOCK = 512
AHEAD = 2


def column_blocks(width):
    sizes = [FIRST] + [min(BLOCK, width - at) for at in range(FIRST, width, BLOCK)]
    return [(sum(sizes[:i]), size) for i, size in enumerate(sizes)]


def first_kernel(w_ref, head_ref, sem):
    copy = pltpu.make_async_copy(w_ref.at[:, pl.ds(0, head_ref.shape[1])], head_ref, sem)
    copy.start()
    copy.wait()


def first_block(head_weight):
    depth, width = head_weight.shape
    return pl.pallas_call(
        first_kernel,
        in_specs=[HBM],
        out_specs=VMEM,
        out_shape=jax.ShapeDtypeStruct((depth, column_blocks(width)[0][1]), head_weight.dtype),
        scratch_shapes=[pltpu.SemaphoreType.DMA],
        compiler_params=params(2),
        cost_estimate=cost(0, 4 * depth * BLOCK),
        name="first_block",
    )(in_hbm(head_weight))


def parts_of(x, count):
    parts = []
    for _ in range(count):
        parts.append(x.astype(jnp.bfloat16).astype(jnp.float32))
        x = x - parts[-1]
    return parts


def student_kernel(meta_ref, *refs):
    own, other = refs[0:RING], refs[RING : 2 * RING]
    w_ref, x_ref, first_ref, s_ref, send_ref = refs[2 * RING : 2 * RING + 5]
    blocks = column_blocks(s_ref.shape[1])
    n = len(blocks)
    heads = refs[2 * RING + 2 : 2 * RING + 3] + refs[2 * RING + 5 : 2 * RING + 4 + n]
    hidden, peaks, totals, t_peaks, t_totals, sem = refs[2 * RING + 4 + n :]
    rows, width = s_ref.shape
    tiles_x, shards = x_ref.shape[0], x_ref.shape[2] // width
    share = own[0].shape[1]
    core = meta_ref[0]
    copies = [None] + [
        pltpu.make_async_copy(w_ref.at[:, pl.ds(first, size)], heads[k], sem.at[k])
        for k, (first, size) in enumerate(blocks)
        if k > 0
    ]
    for copy in copies[1 : 1 + AHEAD]:
        copy.start()
    for i in range(CHIPS):
        at = slice((i % RING) * rows, (i % RING + 1) * rows)
        chip = meta_ref[3 + i] * 2
        hidden[:, pl.ds(pl.multiple_of((chip + core) * share, share), share)] = own[i // RING][at, :]
        hidden[:, pl.ds(pl.multiple_of((chip + 1 - core) * share, share), share)] = other[i // RING][at, :]

    def add(tiles, peak_ref, total_ref, k):
        peak = functools.reduce(jnp.maximum, tiles)
        if k > 0:
            old = peak_ref[...]
            peak = jnp.maximum(peak, old)
        total = functools.reduce(jnp.add, [jnp.exp(x - peak) for x in tiles])
        total_ref[...] = total if k == 0 else total + total_ref[...] * jnp.exp(old - peak)
        peak_ref[...] = peak

    def tally(k):
        first, size = blocks[k]
        add([s_ref[:, j : j + 128] for j in range(first, first + size, 128)], peaks, totals, k)

    def tally_teacher(k):
        first, size = blocks[k]
        tiles = []
        for i in range(tiles_x):
            for j in range(shards):
                x = x_ref[i, :, j * width + first : j * width + first + size]
                send_ref[i * shards + j, :, first : first + size] = x
                x = x.astype(jnp.float32)
                tiles += [x[:, c : c + 128] for c in range(0, size, 128)]
        add(tiles, t_peaks, t_totals, k)

    for k, (first, size) in enumerate(blocks):
        if k > 0:
            copies[k].wait()
            if k + AHEAD < n:
                copies[k + AHEAD].start()

        @pl.when(core >= 0)
        def _():
            s_ref[:, first : first + size] = jnp.dot(
                hidden[...], heads[k][...], preferred_element_type=jnp.float32
            )
            tally_teacher(k)
            if k > 0:
                tally(k - 1)

    tally(n - 1)
    peak = jnp.max(peaks[...], axis=1, keepdims=True)
    lse = peak + jnp.log(jnp.sum(totals[...] * jnp.exp(peaks[...] - peak), axis=1, keepdims=True))
    t_peak = jnp.max(t_peaks[...], axis=1, keepdims=True)
    t_lse = t_peak + jnp.log(jnp.sum(t_totals[...] * jnp.exp(t_peaks[...] - t_peak), axis=1, keepdims=True))
    row = lax.broadcasted_iota(jnp.int32, (8, 128), 0)
    lane = lax.broadcasted_iota(jnp.int32, (8, 128), 1)
    lines = [part[:, h : h + 128] for part in parts_of(to_row(lse), 3) for h in range(0, rows, 128)]
    t_line = jnp.zeros((8, 128), jnp.float32)
    for k, part in enumerate(parts_of(t_lse, 3)):
        t_line = jnp.where(lane == k * 8 + row, part, t_line)
    lines.append(jnp.sum(t_line, axis=0, keepdims=True))
    stat = jnp.zeros((8, 128), jnp.float32)
    for k, line in enumerate(lines):
        stat = jnp.where(row == k, line, stat)
    stat = stat.astype(jnp.bfloat16)
    for i in range(send_ref.shape[0]):
        send_ref[i, :, width:] = stat


def student_logits(meta, own, other, head_weight, teacher_rows, first):
    depth, width = head_weight.shape
    rows = own[0].shape[0] // RING
    blocks = column_blocks(width)
    return pl.pallas_call(
        student_kernel,
        in_specs=[SMEM] + [VMEM] * (2 * RING) + [HBM, VMEM, VMEM],
        out_specs=[VMEM] * (1 + len(blocks)),
        out_shape=[
            jax.ShapeDtypeStruct((rows, width), jnp.float32),
            jax.ShapeDtypeStruct((2 * CHIPS, 8, width + 128), jnp.bfloat16),
        ]
        + [jax.ShapeDtypeStruct((depth, size), jnp.bfloat16) for _, size in blocks[1:]],
        scratch_shapes=[
            pltpu.VMEM((rows, depth), jnp.bfloat16),
            pltpu.VMEM((rows, 128), jnp.float32),
            pltpu.VMEM((rows, 128), jnp.float32),
            pltpu.VMEM((8, 128), jnp.float32),
            pltpu.VMEM((8, 128), jnp.float32),
            pltpu.SemaphoreType.DMA((len(blocks),)),
        ],
        compiler_params=params(10),
        cost_estimate=cost(2 * rows * depth * width, 2 * depth * width),
        name="student_logits",
    )(meta, *own, *other, in_hbm(head_weight), teacher_rows, in_vmem(first))


def merged(stats, rows):
    halves = rows // 128
    line = lambda x, k: jnp.concatenate([x[k * halves + h : k * halves + h + 1] for h in range(halves)], axis=1)
    lses = [(line(x, 0) + line(x, 1)) + line(x, 2) for x in stats]
    top = functools.reduce(jnp.maximum, lses)
    total = functools.reduce(jnp.add, [jnp.exp(x - top) for x in lses])
    teacher = jnp.concatenate([x[3 * halves : 3 * halves + 1] for x in stats], axis=0)
    teacher = jnp.broadcast_to(teacher[:, None, :], (len(stats), 8, 128)).reshape(rows, 128)
    row = lax.broadcasted_iota(jnp.int32, (rows, 128), 0)
    lane = lax.broadcasted_iota(jnp.int32, (rows, 128), 1)
    mine = jnp.logical_and(lane < 24, lax.rem(lane, 8) == lax.rem(row, 8))
    return top + jnp.log(total), jnp.sum(jnp.where(mine, teacher, 0.0), axis=1, keepdims=True)


def head_rows(head, core, chips):
    depth, size = head.shape
    share = depth // CHIPS // 2
    return head.reshape(CHIPS, 2, share, size)[chips, core].reshape(-1, size)


def grad_kernel(meta_ref, x_ref, s_ref, id_ref, weight_ref, *refs):
    blocks = column_blocks(s_ref.shape[1])
    heads = refs[: len(blocks)]
    grad_ref, part_ref, tail_ref, column, cross, picked, total = refs[len(blocks) :]
    rows, width = s_ref.shape
    stats = [x_ref[i, :, width:].astype(jnp.float32) for i in range(x_ref.shape[0])]
    student_row, teacher_column = merged(stats, rows)
    column[:, 0:1] = to_column(student_row)
    column[:, 1:2] = teacher_column
    column[:, 2:3] = to_column(weight_ref[...])
    column[:, 3:4] = to_column(id_ref[...].astype(jnp.float32))
    lane = lax.broadcasted_iota(jnp.int32, (ROWS, 128), 1)

    steps = [
        (k, first + low, low, min(STEP, size - low))
        for k, (first, size) in enumerate(blocks)
        for low in range(0, size, STEP)
    ]
    for k, (block, first, low, size) in enumerate(steps):
        for r in range(0, rows, ROWS):
            at = slice(r, r + ROWS)
            student_lse, teacher_lse, weight = column[at, 0:1], column[at, 1:2], column[at, 2:3]
            target = column[at, 3:4].astype(jnp.int32) - meta_ref[1]
            gap = jnp.zeros((ROWS, 128), jnp.float32) if k == 0 else cross[at, :]
            pick = jnp.zeros((ROWS, 128), jnp.float32) if k == 0 else picked[at, :]
            for j in range(first, first + size, 128):
                cols = slice(j, j + 128)
                student_logp = s_ref[at, cols] - student_lse
                teacher = x_ref[r // 8 : (r + ROWS) // 8, :, cols].astype(jnp.float32).reshape(ROWS, 128)
                teacher_logp = teacher - teacher_lse
                student_prob = jnp.exp(student_logp)
                teacher_prob = jnp.exp(teacher_logp)
                hit = lane == target - j
                onehot = jnp.where(hit, 1.0, 0.0)
                gap += teacher_prob * (teacher_logp - student_logp)
                pick += jnp.where(hit, -student_logp, 0.0)
                grad = weight * ((student_prob - teacher_prob) + CE_WEIGHT * (student_prob - onehot))
                grad_ref[at, cols] = grad.astype(jnp.bfloat16)
            cross[at, :] = gap
            picked[at, :] = pick
        out = lax.dot_general(
            head_rows(heads[block], 1 - meta_ref[0], slice(0, CHIPS))[:, low : low + size],
            grad_ref[:, first : first + size],
            (((1,), (1,)), ((), ())),
            preferred_element_type=jnp.float32,
        )
        if k == 0:
            total[...] = out
        elif k + 1 < len(steps):
            total[...] += out
        else:
            part_ref[...] = (total[...] + out).astype(jnp.bfloat16).reshape(part_ref.shape)

    gap = to_row(jnp.sum(cross[...], axis=1, keepdims=True))
    pick = to_row(jnp.sum(picked[...], axis=1, keepdims=True))
    row = lax.broadcasted_iota(jnp.int32, tail_ref.shape, 0)
    tail = jnp.zeros(tail_ref.shape, jnp.float32)
    for k, line in enumerate(parts_of(gap, 3) + parts_of(pick, 3)):
        tail = jnp.where(row == k, line, tail)
    tail_ref[...] = tail.astype(jnp.bfloat16)


def logit_grad(meta, teacher, student, ids, weights, heads):
    rows, width = student.shape
    depth = heads[0].shape[0]
    share = depth // CHIPS // 2
    return pl.pallas_call(
        grad_kernel,
        in_specs=[SMEM] + [VMEM] * (4 + len(heads)),
        out_specs=[VMEM] * 3,
        out_shape=[
            jax.ShapeDtypeStruct((rows, width), jnp.bfloat16),
            jax.ShapeDtypeStruct((CHIPS, share, rows), jnp.bfloat16),
            jax.ShapeDtypeStruct((TAIL, rows), jnp.bfloat16),
        ],
        scratch_shapes=[
            pltpu.VMEM((rows, 128), jnp.float32),
            pltpu.VMEM((rows, 128), jnp.float32),
            pltpu.VMEM((rows, 128), jnp.float32),
            pltpu.VMEM((CHIPS * share, rows), jnp.float32),
        ],
        compiler_params=params(14),
        cost_estimate=cost(rows * depth * width, depth * width),
        name="logit_grad",
    )(meta, teacher, student, ids, weights, *[in_vmem(x) for x in heads])


CHIP_BLOCK = 4
STEP = 256


def own_kernel(meta_ref, grad_ref, *refs):
    heads, part_ref = refs[:-1], refs[-1]
    chips, share, rows = part_ref.shape
    for i in range(0, chips, CHIP_BLOCK):
        total = 0.0
        for k, (first, size) in enumerate(column_blocks(grad_ref.shape[1])):
            total += lax.dot_general(
                head_rows(heads[k], meta_ref[0], slice(i, i + CHIP_BLOCK)),
                grad_ref[:, first : first + size],
                (((1,), (1,)), ((), ())),
                preferred_element_type=jnp.float32,
            )
        part_ref[i : i + CHIP_BLOCK] = total.astype(jnp.bfloat16).reshape(CHIP_BLOCK, share, rows)


def own_share(meta, grad, heads):
    rows, width = grad.shape
    depth = heads[0].shape[0]
    share = depth // CHIPS // 2
    return pl.pallas_call(
        own_kernel,
        in_specs=[SMEM] + [VMEM] * (1 + len(heads)),
        out_specs=VMEM,
        out_shape=jax.ShapeDtypeStruct((CHIPS, share, rows), jnp.bfloat16),
        compiler_params=params(8),
        cost_estimate=cost(rows * depth * width, depth * width),
        name="own_share",
    )(meta, grad, *[in_vmem(x) for x in heads])


def join_kernel(a_ref, b_ref, ta_ref, tb_ref, o_ref):
    share = a_ref.shape[1]
    total = a_ref[...].astype(jnp.float32) + b_ref[...].astype(jnp.float32)
    o_ref[:, 0:share, :] = total.astype(jnp.bfloat16)
    tail = jnp.concatenate(
        [ta_ref[...].astype(jnp.float32)[0 : TAIL // 2], tb_ref[...].astype(jnp.float32)[0 : TAIL // 2]]
    ).astype(jnp.bfloat16)
    for i in range(o_ref.shape[0]):
        o_ref[i, share : share + TAIL, :] = tail


def join(a, b, tail_a, tail_b):
    chips, share, rows = a.shape
    block = pl.BlockSpec((CHIP_BLOCK, share, rows), lambda i: (i, 0, 0))
    tail = pl.BlockSpec((TAIL, rows), lambda i: (0, 0))
    return pl.pallas_call(
        join_kernel,
        grid=(chips // CHIP_BLOCK,),
        in_specs=[block, block, tail, tail],
        out_specs=pl.BlockSpec((CHIP_BLOCK, share + TAIL, rows), lambda i: (i, 0, 0)),
        out_shape=jax.ShapeDtypeStruct((chips, share + TAIL, rows), jnp.bfloat16),
        compiler_params=params(16),
        name="chip_sum",
    )(a, b, tail_a, tail_b)


def final_kernel(x_ref, div_ref, ce_ref, o_ref):
    chips = x_ref.shape[0]
    share = x_ref.shape[1] - TAIL
    total = x_ref[0, 0:share, :].astype(jnp.float32)
    for i in range(1, chips):
        total += x_ref[i, 0:share, :].astype(jnp.float32)
    o_ref[...] = total.astype(jnp.bfloat16)
    div = jnp.zeros(div_ref.shape, jnp.float32)
    ce = jnp.zeros(ce_ref.shape, jnp.float32)
    for i in range(chips):
        tail = x_ref[i, share : share + TAIL, :].astype(jnp.float32)
        line = lambda k: tail[k : k + 1]
        value = lambda k: (line(k) + line(k + 1)) + line(k + 2)
        half = TAIL // 2
        div += value(0) + value(half)
        ce += value(3) + value(half + 3)
    div_ref[...] = div
    ce_ref[...] = ce


def final(blocks):
    chips, height, rows = blocks.shape
    return pl.pallas_call(
        final_kernel,
        out_shape=[
            jax.ShapeDtypeStruct((1, rows), jnp.float32),
            jax.ShapeDtypeStruct((1, rows), jnp.float32),
            jax.ShapeDtypeStruct((height - TAIL, rows), jnp.bfloat16),
        ],
        compiler_params=params(16),
        name="final_sum",
    )(blocks)


def on_device(hidden, head_weight, teacher_logits, token_ids, token_weight):
    rows, share = hidden.shape
    depth, width = head_weight.shape
    me = lax.axis_index("vocab")
    core, chip = me % 2, me // 2
    y, z = chip // RING, chip % RING
    sources = [((y - dy) % RING) * RING + (z - dz) % RING for dy in SHIFTS for dz in SHIFTS]

    meta = jnp.stack([core, me * width, me] + sources).astype(jnp.int32)

    along_z = jnp.concatenate(from_ring(hidden, "dz"), axis=0)
    blocks = jnp.transpose(teacher_logits, (1, 0, 2)).reshape(rows // 8, -1)
    blocks = lax.all_to_all(after(blocks, meta), "tok", 0, 0, tiled=True)
    own = from_ring(along_z, "dy")
    other = [swap_core(x) for x in own]
    blocks = blocks.reshape(-1, 8, blocks.shape[1])
    first = first_block(after(head_weight, blocks))
    student, send, *heads = student_logits(meta, own, other, head_weight, blocks, first)
    heads = [first] + heads

    teacher = lax.all_to_all(send, "vocab", 0, 0, tiled=True)
    grad, part, tail = logit_grad(
        meta, teacher, student, token_ids.reshape(1, rows), token_weight.reshape(1, rows), heads
    )
    from_core, from_tail = swap_core(part), swap_core(tail)
    mine = own_share(meta, grad, heads)
    summed = join(mine, from_core, tail, from_tail)

    same_core = [[member(i // RING, i % RING, c) for i in range(CHIPS)] for c in range(2)]
    blocks = lax.all_to_all(
        summed.reshape(CHIPS * (share + TAIL), rows), "vocab", 0, 0, axis_index_groups=same_core, tiled=True
    )
    divergence, cross_entropy, hidden_grad = final(blocks.reshape(CHIPS, share + TAIL, rows))
    return divergence.reshape(rows), cross_entropy.reshape(rows), hidden_grad


def solution(mesh):
    return jax.shard_map(
        on_device,
        mesh=mesh,
        in_specs=(P("tok", "vocab"), P(None, "vocab"), P("vocab", None, "tok"), P("tok"), P("tok")),
        out_specs=(P("tok"), P("tok"), P("vocab", "tok")),
        check_vma=False,
    )
```

```python
import functools

import jax
import jax.numpy as jnp
from jax import lax
from jax.experimental import pallas as pl
from jax.experimental.pallas import tpu as pltpu
from jax.sharding import PartitionSpec as P

CE_WEIGHT = 0.5
RING = 4
CHIPS = RING * RING
SHIFTS = (0, 1, -1, 2)
MIB = 1 << 20
SMEM = pl.BlockSpec(memory_space=pltpu.SMEM)
VMEM = pl.BlockSpec(memory_space=pltpu.VMEM)
HBM = pl.BlockSpec(memory_space=pltpu.HBM)
TAIL = 16


def params(limit):
    return pltpu.CompilerParams(vmem_limit_bytes=limit * MIB)


def cost(flops, read):
    return pl.CostEstimate(flops=flops, bytes_accessed=read, transcendentals=0)


def in_vmem(x):
    return pltpu.with_memory_space_constraint(x, pltpu.VMEM)


def in_hbm(x):
    return pltpu.with_memory_space_constraint(x, pltpu.HBM)


def after(x, *others):
    return lax.optimization_barrier((x,) + others)[0]


def member(y, z, core):
    return ((y % RING) * RING + z % RING) * 2 + core % 2


def moves(dy=0, dz=0, dcore=0):
    return [
        (member(y, z, c), member(y + dy, z + dz, c + dcore))
        for y in range(RING)
        for z in range(RING)
        for c in range(2)
    ]


def swap_core(x):
    return lax.ppermute(x, "vocab", moves(dcore=1))


def from_ring(x, axis):
    return [x] + [lax.ppermute(x, "vocab", moves(**{axis: d})) for d in SHIFTS[1:]]


def eye(n):
    return lax.broadcasted_iota(jnp.int32, (n, n), 0) == lax.broadcasted_iota(jnp.int32, (n, n), 1)


def to_column(row):
    n = row.shape[1]
    return jnp.sum(jnp.where(eye(n), row, 0.0), axis=1, keepdims=True)


def to_row(column):
    n = column.shape[0]
    return jnp.sum(jnp.where(eye(n), column, 0.0), axis=0, keepdims=True)


ROWS = 32
BLOCK = 512
AHEAD = 2


def column_blocks(width):
    return [(first, min(BLOCK, width - first)) for first in range(0, width, BLOCK)]


def parts_of(x, count):
    parts = []
    for _ in range(count):
        parts.append(x.astype(jnp.bfloat16).astype(jnp.float32))
        x = x - parts[-1]
    return parts


def student_kernel(meta_ref, *refs):
    blocks = column_blocks(refs[2 * RING + 2].shape[1])
    n = len(blocks)
    own, other = refs[0:RING], refs[RING : 2 * RING]
    w_ref, x_ref, s_ref, send_ref = refs[2 * RING : 2 * RING + 4]
    heads = refs[2 * RING + 4 : 2 * RING + 4 + n]
    hidden, peaks, totals, t_peaks, t_totals, sem = refs[2 * RING + 4 + n :]
    rows, width = s_ref.shape
    tiles_x, shards = x_ref.shape[0], x_ref.shape[2] // width
    share = own[0].shape[1]
    core = meta_ref[0]
    copies = [
        pltpu.make_async_copy(w_ref.at[:, pl.ds(first, size)], heads[k], sem.at[k])
        for k, (first, size) in enumerate(blocks)
    ]
    for copy in copies[:AHEAD]:
        copy.start()
    for i in range(CHIPS):
        at = slice((i % RING) * rows, (i % RING + 1) * rows)
        chip = meta_ref[3 + i] * 2
        hidden[:, pl.ds(pl.multiple_of((chip + core) * share, share), share)] = own[i // RING][at, :]
        hidden[:, pl.ds(pl.multiple_of((chip + 1 - core) * share, share), share)] = other[i // RING][at, :]

    def add(tiles, peak_ref, total_ref, k):
        peak = functools.reduce(jnp.maximum, tiles)
        if k > 0:
            old = peak_ref[...]
            peak = jnp.maximum(peak, old)
        total = functools.reduce(jnp.add, [jnp.exp(x - peak) for x in tiles])
        total_ref[...] = total if k == 0 else total + total_ref[...] * jnp.exp(old - peak)
        peak_ref[...] = peak

    def tally(k):
        first, size = blocks[k]
        add([s_ref[:, j : j + 128] for j in range(first, first + size, 128)], peaks, totals, k)

    def tally_teacher(k):
        first, size = blocks[k]
        tiles = []
        for i in range(tiles_x):
            for j in range(shards):
                x = x_ref[i, :, j * width + first : j * width + first + size]
                send_ref[i * shards + j, :, first : first + size] = x
                x = x.astype(jnp.float32)
                tiles += [x[:, c : c + 128] for c in range(0, size, 128)]
        add(tiles, t_peaks, t_totals, k)

    for k, (first, size) in enumerate(blocks):
        copies[k].wait()
        if k + AHEAD < n:
            copies[k + AHEAD].start()

        @pl.when(core >= 0)
        def _():
            s_ref[:, first : first + size] = jnp.dot(
                hidden[...], heads[k][...], preferred_element_type=jnp.float32
            )
            tally_teacher(k)
            if k > 0:
                tally(k - 1)

    tally(n - 1)
    peak = jnp.max(peaks[...], axis=1, keepdims=True)
    lse = peak + jnp.log(jnp.sum(totals[...] * jnp.exp(peaks[...] - peak), axis=1, keepdims=True))
    t_peak = jnp.max(t_peaks[...], axis=1, keepdims=True)
    t_lse = t_peak + jnp.log(jnp.sum(t_totals[...] * jnp.exp(t_peaks[...] - t_peak), axis=1, keepdims=True))
    row = lax.broadcasted_iota(jnp.int32, (8, 128), 0)
    lane = lax.broadcasted_iota(jnp.int32, (8, 128), 1)
    lines = [part[:, h : h + 128] for part in parts_of(to_row(lse), 3) for h in range(0, rows, 128)]
    t_line = jnp.zeros((8, 128), jnp.float32)
    for k, part in enumerate(parts_of(t_lse, 3)):
        t_line = jnp.where(lane == k * 8 + row, part, t_line)
    lines.append(jnp.sum(t_line, axis=0, keepdims=True))
    stat = jnp.zeros((8, 128), jnp.float32)
    for k, line in enumerate(lines):
        stat = jnp.where(row == k, line, stat)
    stat = stat.astype(jnp.bfloat16)
    for i in range(send_ref.shape[0]):
        send_ref[i, :, width:] = stat


def student_logits(meta, own, other, head_weight, teacher_rows):
    depth, width = head_weight.shape
    rows = own[0].shape[0] // RING
    blocks = column_blocks(width)
    return pl.pallas_call(
        student_kernel,
        in_specs=[SMEM] + [VMEM] * (2 * RING) + [HBM, VMEM],
        out_specs=[VMEM] * (2 + len(blocks)),
        out_shape=[
            jax.ShapeDtypeStruct((rows, width), jnp.float32),
            jax.ShapeDtypeStruct((2 * CHIPS, 8, width + 128), jnp.bfloat16),
        ]
        + [jax.ShapeDtypeStruct((depth, size), jnp.bfloat16) for _, size in blocks],
        scratch_shapes=[
            pltpu.VMEM((rows, depth), jnp.bfloat16),
            pltpu.VMEM((rows, 128), jnp.float32),
            pltpu.VMEM((rows, 128), jnp.float32),
            pltpu.VMEM((8, 128), jnp.float32),
            pltpu.VMEM((8, 128), jnp.float32),
            pltpu.SemaphoreType.DMA((len(blocks),)),
        ],
        compiler_params=params(10),
        cost_estimate=cost(2 * rows * depth * width, 2 * depth * width),
        name="student_logits",
    )(meta, *own, *other, in_hbm(head_weight), teacher_rows)


def merged(stats, rows):
    halves = rows // 128
    line = lambda x, k: jnp.concatenate([x[k * halves + h : k * halves + h + 1] for h in range(halves)], axis=1)
    lses = [(line(x, 0) + line(x, 1)) + line(x, 2) for x in stats]
    top = functools.reduce(jnp.maximum, lses)
    total = functools.reduce(jnp.add, [jnp.exp(x - top) for x in lses])
    teacher = jnp.concatenate([x[3 * halves : 3 * halves + 1] for x in stats], axis=0)
    teacher = jnp.broadcast_to(teacher[:, None, :], (len(stats), 8, 128)).reshape(rows, 128)
    row = lax.broadcasted_iota(jnp.int32, (rows, 128), 0)
    lane = lax.broadcasted_iota(jnp.int32, (rows, 128), 1)
    mine = jnp.logical_and(lane < 24, lax.rem(lane, 8) == lax.rem(row, 8))
    return top + jnp.log(total), jnp.sum(jnp.where(mine, teacher, 0.0), axis=1, keepdims=True)


def head_rows(head, core, chips):
    depth, size = head.shape
    share = depth // CHIPS // 2
    return head.reshape(CHIPS, 2, share, size)[chips, core].reshape(-1, size)


def grad_kernel(meta_ref, x_ref, s_ref, id_ref, weight_ref, *refs):
    blocks = column_blocks(s_ref.shape[1])
    heads = refs[: len(blocks)]
    grad_ref, part_ref, column, cross, picked, total = refs[len(blocks) :]
    rows, width = s_ref.shape
    stats = [x_ref[i, :, width:].astype(jnp.float32) for i in range(x_ref.shape[0])]
    student_row, teacher_column = merged(stats, rows)
    column[:, 0:1] = to_column(student_row)
    column[:, 1:2] = teacher_column
    column[:, 2:3] = to_column(weight_ref[...])
    column[:, 3:4] = to_column(id_ref[...].astype(jnp.float32))
    lane = lax.broadcasted_iota(jnp.int32, (ROWS, 128), 1)

    steps = [
        (k, first + low, low, min(STEP, size - low))
        for k, (first, size) in enumerate(blocks)
        for low in range(0, size, STEP)
    ]
    for k, (block, first, low, size) in enumerate(steps):
        for r in range(0, rows, ROWS):
            at = slice(r, r + ROWS)
            student_lse, teacher_lse, weight = column[at, 0:1], column[at, 1:2], column[at, 2:3]
            target = column[at, 3:4].astype(jnp.int32) - meta_ref[1]
            target_weight = CE_WEIGHT * weight
            gap = jnp.zeros((ROWS, 128), jnp.float32) if k == 0 else cross[at, :]
            pick = jnp.zeros((ROWS, 128), jnp.float32) if k == 0 else picked[at, :]
            for j in range(first, first + size, 128):
                cols = slice(j, j + 128)
                student_logp = s_ref[at, cols] - student_lse
                teacher = x_ref[r // 8 : (r + ROWS) // 8, :, cols].astype(jnp.float32).reshape(ROWS, 128)
                teacher_logp = teacher - teacher_lse
                student_prob = jnp.exp(student_logp)
                teacher_prob = jnp.exp(teacher_logp)
                hit = lane == target - j
                gap += teacher_prob * (teacher_logp - student_logp)
                pick = jnp.where(hit, student_logp, pick)
                grad = weight * ((1.0 + CE_WEIGHT) * student_prob - teacher_prob) - jnp.where(hit, target_weight, 0.0)
                grad_ref[at, cols] = grad.astype(jnp.bfloat16)
            cross[at, :] = gap
            picked[at, :] = pick
        out = lax.dot_general(
            head_rows(heads[block], 1 - meta_ref[0], slice(0, CHIPS))[:, low : low + size],
            grad_ref[:, first : first + size],
            (((1,), (1,)), ((), ())),
            preferred_element_type=jnp.float32,
        )
        if k == 0:
            total[...] = out
        elif k + 1 < len(steps):
            total[...] += out
        else:
            part_ref[0 : total.shape[0], :] = (total[...] + out).astype(jnp.bfloat16)

    gap = to_row(jnp.sum(cross[...], axis=1, keepdims=True))
    pick = -to_row(jnp.sum(picked[...], axis=1, keepdims=True))
    row = lax.broadcasted_iota(jnp.int32, (TAIL, rows), 0)
    tail = jnp.zeros((TAIL, rows), jnp.float32)
    for k, line in enumerate(parts_of(gap, 3) + parts_of(pick, 3)):
        tail = jnp.where(row == k, line, tail)
    part_ref[total.shape[0] :, :] = tail.astype(jnp.bfloat16)


def logit_grad(meta, teacher, student, ids, weights, heads):
    rows, width = student.shape
    depth = heads[0].shape[0]
    share = depth // CHIPS // 2
    return pl.pallas_call(
        grad_kernel,
        in_specs=[SMEM] + [VMEM] * (4 + len(heads)),
        out_specs=[VMEM] * 2,
        out_shape=[
            jax.ShapeDtypeStruct((rows, width), jnp.bfloat16),
            jax.ShapeDtypeStruct((CHIPS * share + TAIL, rows), jnp.bfloat16),
        ],
        scratch_shapes=[
            pltpu.VMEM((rows, 128), jnp.float32),
            pltpu.VMEM((rows, 128), jnp.float32),
            pltpu.VMEM((rows, 128), jnp.float32),
            pltpu.VMEM((CHIPS * share, rows), jnp.float32),
        ],
        compiler_params=params(14),
        cost_estimate=cost(rows * depth * width, depth * width),
        name="logit_grad",
    )(meta, teacher, student, ids, weights, *[in_vmem(x) for x in heads])


CHIP_BLOCK = 4
STEP = 256


def own_kernel(meta_ref, grad_ref, *refs):
    heads, part_ref = refs[:-1], refs[-1]
    chips, share, rows = part_ref.shape
    for i in range(0, chips, CHIP_BLOCK):
        total = 0.0
        for k, (first, size) in enumerate(column_blocks(grad_ref.shape[1])):
            total += lax.dot_general(
                head_rows(heads[k], meta_ref[0], slice(i, i + CHIP_BLOCK)),
                grad_ref[:, first : first + size],
                (((1,), (1,)), ((), ())),
                preferred_element_type=jnp.float32,
            )
        part_ref[i : i + CHIP_BLOCK] = total.astype(jnp.bfloat16).reshape(CHIP_BLOCK, share, rows)


def own_share(meta, grad, heads):
    rows, width = grad.shape
    depth = heads[0].shape[0]
    share = depth // CHIPS // 2
    return pl.pallas_call(
        own_kernel,
        in_specs=[SMEM] + [VMEM] * (1 + len(heads)),
        out_specs=VMEM,
        out_shape=jax.ShapeDtypeStruct((CHIPS, share, rows), jnp.bfloat16),
        compiler_params=params(8),
        cost_estimate=cost(rows * depth * width, depth * width),
        name="own_share",
    )(meta, grad, *[in_vmem(x) for x in heads])


def join_kernel(a_ref, b_ref, ta_ref, tb_ref, o_ref):
    blocks, share, rows = a_ref.shape
    total = a_ref[...].astype(jnp.float32) + b_ref[...].reshape(blocks, share, rows).astype(jnp.float32)
    o_ref[:, 0:share, :] = total.astype(jnp.bfloat16)
    tail = jnp.concatenate(
        [ta_ref[...].astype(jnp.float32)[0 : TAIL // 2], tb_ref[...].astype(jnp.float32)[0 : TAIL // 2]]
    ).astype(jnp.bfloat16)
    for i in range(blocks):
        o_ref[i, share : share + TAIL, :] = tail


def join(mine, sent, received):
    chips, share, rows = mine.shape
    tail = pl.BlockSpec((TAIL, rows), lambda i: (chips * share // TAIL, 0))
    return pl.pallas_call(
        join_kernel,
        grid=(chips // CHIP_BLOCK,),
        in_specs=[
            pl.BlockSpec((CHIP_BLOCK, share, rows), lambda i: (i, 0, 0)),
            pl.BlockSpec((CHIP_BLOCK * share, rows), lambda i: (i, 0)),
            tail,
            tail,
        ],
        out_specs=pl.BlockSpec((CHIP_BLOCK, share + TAIL, rows), lambda i: (i, 0, 0)),
        out_shape=jax.ShapeDtypeStruct((chips, share + TAIL, rows), jnp.bfloat16),
        compiler_params=params(16),
        name="chip_sum",
    )(mine, received, sent, received)


def final_kernel(x_ref, div_ref, ce_ref, o_ref):
    chips = x_ref.shape[0]
    share = x_ref.shape[1] - TAIL
    total = x_ref[0, 0:share, :].astype(jnp.float32)
    for i in range(1, chips):
        total += x_ref[i, 0:share, :].astype(jnp.float32)
    o_ref[...] = total.astype(jnp.bfloat16)
    div = jnp.zeros(div_ref.shape, jnp.float32)
    ce = jnp.zeros(ce_ref.shape, jnp.float32)
    for i in range(chips):
        tail = x_ref[i, share : share + TAIL, :].astype(jnp.float32)
        line = lambda k: tail[k : k + 1]
        value = lambda k: (line(k) + line(k + 1)) + line(k + 2)
        half = TAIL // 2
        div += value(0) + value(half)
        ce += value(3) + value(half + 3)
    div_ref[...] = div
    ce_ref[...] = ce


def final(blocks):
    chips, height, rows = blocks.shape
    return pl.pallas_call(
        final_kernel,
        out_shape=[
            jax.ShapeDtypeStruct((1, rows), jnp.float32),
            jax.ShapeDtypeStruct((1, rows), jnp.float32),
            jax.ShapeDtypeStruct((height - TAIL, rows), jnp.bfloat16),
        ],
        compiler_params=params(16),
        name="final_sum",
    )(blocks)


def on_device(hidden, head_weight, teacher_logits, token_ids, token_weight):
    rows, share = hidden.shape
    depth, width = head_weight.shape
    me = lax.axis_index("vocab")
    core, chip = me % 2, me // 2
    y, z = chip // RING, chip % RING
    sources = [((y - dy) % RING) * RING + (z - dz) % RING for dy in SHIFTS for dz in SHIFTS]

    meta = jnp.stack([core, me * width, me] + sources).astype(jnp.int32)

    along_z = jnp.concatenate(from_ring(hidden, "dz"), axis=0)
    blocks = jnp.transpose(teacher_logits, (1, 0, 2)).reshape(rows // 8, -1)
    blocks = lax.all_to_all(after(blocks, meta), "tok", 0, 0, tiled=True)
    own = from_ring(along_z, "dy")
    other = [swap_core(x) for x in own]
    student, send, *heads = student_logits(
        meta, own, other, head_weight, blocks.reshape(-1, 8, blocks.shape[1])
    )

    teacher = lax.all_to_all(send, "vocab", 0, 0, tiled=True)
    grad, part = logit_grad(
        meta, teacher, student, token_ids.reshape(1, rows), token_weight.reshape(1, rows), heads
    )
    from_core = swap_core(part)
    mine = own_share(meta, grad, heads)
    summed = join(mine, part, from_core)

    same_core = [[member(i // RING, i % RING, c) for i in range(CHIPS)] for c in range(2)]
    blocks = lax.all_to_all(
        summed.reshape(CHIPS * (share + TAIL), rows), "vocab", 0, 0, axis_index_groups=same_core, tiled=True
    )
    divergence, cross_entropy, hidden_grad = final(blocks.reshape(CHIPS, share + TAIL, rows))
    return divergence.reshape(rows), cross_entropy.reshape(rows), hidden_grad


def solution(mesh):
    return jax.shard_map(
        on_device,
        mesh=mesh,
        in_specs=(P("tok", "vocab"), P(None, "vocab"), P("vocab", None, "tok"), P("tok"), P("tok")),
        out_specs=(P("tok"), P("tok"), P("vocab", "tok")),
        check_vma=False,
    )
```
